512 devices in a mesh: seq: 128 (over y, z, core), mp: 4 (over x).
Axes of the slice: x: 4, y: 8, z: 8, core: 2. Of those that a mesh axis runs over, the one named last changes fastest.
Arguments:
- layer_input: bfloat16 [16384, 2048], P('seq', 'mp'), may hold values from -6 to 6
- output_grad: bfloat16 [16384, 2048], P('seq', 'mp'), may hold values from -6 to 6
- w_out: bfloat16 [512, 2048], P('mp'), may hold values from -0.125 to 0.125
- query_heads: bfloat16 [4, 16384, 128], P('mp', 'seq'), may hold values from -32 to 32
- key_heads: bfloat16 [4, 16384, 128], P('mp', 'seq'), may hold values from -8 to 8
- value_heads: bfloat16 [4, 16384, 128], P('mp', 'seq'), may hold values from -6 to 6
- cluster_ids: int32 [4, 16384, 1], P('mp', 'seq'), may hold values from 0 to 63, as said below
Outputs:
- query_grad: bfloat16 [4, 16384, 128], P('mp', 'seq')
- key_grad: bfloat16 [4, 16384, 128], P('mp', 'seq')
- value_grad: bfloat16 [4, 16384, 128], P('mp', 'seq')
- weight_grad: float32 [2048, 1536], P('seq', 'mp')
The draws below stay inside these ranges and needn't reach their ends.
Inputs may be any that keep to these rules, and one draw needn't show every extreme that they name: `cluster_ids`: in each head and among each index of seq's 128 tokens, every cluster holds exactly 2 tokens.
All inputs are finite; a program needn't handle non-finite values.
Results may differ from the reference program's by a relative error of at most 0.018.
Values may be sent and summed in bfloat16 or wider, within the bound.
A program may use at most 64 MiB of HBM per device.

```python
import math
import jax
import jax.numpy as jnp
from jax import lax

D = 2048
HD = 128
CLUSTERS = 64
TOK_DEV = 128
HEADS = 4
MOST = 2
TOKENS = 16384
N_SEQ = 128


def cluster_layout(key):
    blocks = HEADS * (TOKENS // TOK_DEV)
    block_keys = jax.random.split(jax.random.fold_in(key, 501), blocks)
    slot_table = jnp.arange(CLUSTERS * MOST, dtype=jnp.int32) // MOST

    def one_block(sub_key):
        first_key, second_key, third_key = jax.random.split(sub_key, 3)
        full_cluster = jax.random.randint(first_key, (), 0, CLUSTERS)
        shuffle = jax.random.permutation(second_key, CLUSTERS * MOST)
        shuffled = slot_table[shuffle]
        priority = jnp.where(shuffled == full_cluster, 0, CLUSTERS * MOST) + jnp.arange(CLUSTERS * MOST, dtype=jnp.int32)
        chosen = shuffled[jnp.argsort(priority)][:TOK_DEV]
        return (jax.random.permutation(third_key, chosen), full_cluster)
    members, full_cluster = jax.vmap(one_block)(block_keys)
    return members.reshape(HEADS, TOKENS, 1)


def draw_cluster_ids(key, part):
    members = cluster_layout(key)
    return members.astype(jnp.int32)


def draw_query_heads(key, part):
    key = jax.random.fold_in(key, 11)
    first_key = jax.random.fold_in(key, 0)
    values = jnp.clip(jax.random.normal(first_key, (HEADS, TOKENS, HD)), -4.0, 4.0)
    return values.astype(jnp.bfloat16)


def draw_key_heads(key, part):
    key = jax.random.fold_in(key, 12)
    first_key = jax.random.fold_in(key, 0)
    values = jnp.clip(jax.random.normal(first_key, (HEADS, TOKENS, HD)), -4.0, 4.0)
    return values.astype(jnp.bfloat16)


def block_levels(rng, extent, cuts, low, high):
    loudness = 1.0
    for axis_at, shards_of in cuts:
        steps = jax.random.uniform(jax.random.fold_in(jax.random.fold_in(rng, 6), axis_at), (shards_of,), jnp.float32, low / len(cuts), high / len(cuts))
        loudness = loudness * jnp.repeat(jnp.exp(steps), extent[axis_at] // shards_of).reshape((-1,) + (1,) * (len(extent) - 1 - axis_at))
    return loudness


def bell_draw(key, shape, deviation, bound, cuts=(), kind=jnp.bfloat16):
    array = deviation * jax.random.normal(key, shape, jnp.float32)
    if cuts:
        array = array * block_levels(key, shape, cuts, -0.22, 0.18)
    return jnp.clip(array, -bound, bound).astype(kind)


def setup_inputs(seed: int = 0) -> dict:
    keys = jax.random.split(jax.random.key(seed), 8)
    return {
        "layer_input": bell_draw(keys[0], (TOKENS, D), 1.0, 6.0, ((0, 128), (1, 4))),
        "output_grad": bell_draw(keys[1], (TOKENS, D), 1.0, 6.0, ((0, 128), (1, 4))),
        "w_out": bell_draw(keys[2], (HEADS * HD, D), D ** -0.5, 0.125, ((0, 4),)),
        "query_heads": draw_query_heads(jax.random.fold_in(keys[7], 71), 0),
        "key_heads": draw_key_heads(jax.random.fold_in(keys[7], 71), 0),
        "value_heads": bell_draw(keys[5], (HEADS, TOKENS, HD), 1.0, 6.0, ((0, 4), (1, 128))),
        "cluster_ids": draw_cluster_ids(jax.random.fold_in(keys[7], 71), 0),
    }


def cluster_grads(packed, slot_live, score_scale):
    query_rows = packed[:, 0:HD]
    key_rows = packed[:, HD:2 * HD]
    value_rows = packed[:, 2 * HD:3 * HD]
    grad_rows = packed[:, 3 * HD:4 * HD]
    place = jnp.arange(packed.shape[0])
    allowed = (place[None, :] <= place[:, None]) & slot_live[None, :] & slot_live[:, None]
    scores = jnp.dot(query_rows, key_rows.T, preferred_element_type=jnp.float32) * score_scale
    scores = jnp.where(allowed, scores, -1e+30)
    row_max = lax.optimization_barrier(jnp.max(scores, axis=1, keepdims=True))
    weights = jnp.exp(scores - row_max)
    probs = jnp.where(allowed, weights / lax.optimization_barrier(jnp.sum(weights, axis=1, keepdims=True)), 0.0)
    probs_low = probs.astype(jnp.bfloat16)
    attended = jnp.dot(probs_low, value_rows, preferred_element_type=jnp.float32)
    row_delta = lax.optimization_barrier(jnp.sum(grad_rows.astype(jnp.float32) * attended, axis=1))
    prob_grad = jnp.dot(grad_rows, value_rows.T, preferred_element_type=jnp.float32)
    dscore = (probs * (prob_grad - row_delta[:, None])).astype(jnp.bfloat16)
    query_part = jnp.dot(dscore, key_rows, preferred_element_type=jnp.float32) * score_scale
    key_part = jnp.dot(dscore.T, query_rows, preferred_element_type=jnp.float32) * score_scale
    value_part = jnp.dot(probs_low.T, grad_rows, preferred_element_type=jnp.float32)
    return jnp.concatenate([query_part, key_part, value_part], axis=1)

def reference(layer_input, output_grad, w_out, query_heads, key_heads, value_heads, cluster_ids):
    score_scale = 1.0 / math.sqrt(HD)
    slot_span = N_SEQ * MOST
    query_list = []
    key_list = []
    value_list = []
    weight_list = []
    for head_index in range(HEADS):
        head_rows = w_out[head_index * HD:(head_index + 1) * HD]
        head_grad = jnp.dot(output_grad, head_rows.T, preferred_element_type=jnp.float32).astype(jnp.bfloat16)
        members = cluster_ids[head_index, :, 0].reshape(N_SEQ, TOK_DEV)
        onehot = (members[:, :, None] == jnp.arange(CLUSTERS, dtype=jnp.int32)[None, None, :]).astype(jnp.int32)
        slot = lax.optimization_barrier(jnp.sum((jnp.cumsum(onehot, axis=1) - onehot) * onehot, axis=2))
        counts = lax.optimization_barrier(jnp.sum(onehot, axis=1))
        target = ((members * N_SEQ + jnp.arange(N_SEQ, dtype=jnp.int32)[:, None]) * MOST + slot).reshape(-1).astype(jnp.int32)
        slot_live = (jnp.arange(MOST, dtype=jnp.int32)[None, None, :] < counts.T[:, :, None]).reshape(CLUSTERS, slot_span)
        packed = jnp.concatenate([query_heads[head_index], key_heads[head_index], value_heads[head_index], head_grad], axis=1)
        buffer = jnp.zeros((CLUSTERS * slot_span, 4 * HD), packed.dtype).at[target].set(packed)
        buffer = buffer.reshape(CLUSTERS, slot_span, 4 * HD)
        grads = lax.map(lambda pair: cluster_grads(pair[0], pair[1], score_scale), (buffer, slot_live))
        token_grads = grads.reshape(CLUSTERS * slot_span, 3 * HD)[target].astype(jnp.bfloat16)
        query_list.append(token_grads[:, 0:HD])
        key_list.append(token_grads[:, HD:2 * HD])
        value_list.append(token_grads[:, 2 * HD:3 * HD])
        weight_list.append(jnp.dot(layer_input.T, token_grads, preferred_element_type=jnp.float32))
    return (jnp.stack(query_list), jnp.stack(key_list), jnp.stack(value_list), jnp.concatenate(weight_list, axis=1))
```

```python
import math

import jax
import jax.numpy as jnp
from jax import lax
from jax.experimental import pallas as pl
from jax.experimental.pallas import tpu as pltpu
from jax.sharding import PartitionSpec as P

MOST = 2
KINDS = 4
MESSAGE = MOST * KINDS
FEATS = 16
MESH = pl.DeviceIdType.MESH
F32 = jnp.float32
BF16 = jnp.bfloat16
NT = (((1,), (1,)), ((), ()))
TN = (((0,), (0,)), ((), ()))


def dot(left, right, dims=(((1,), (0,)), ((), ()))):
    return lax.dot_general(left, right, dims, preferred_element_type=F32)


def iota(shape, dim):
    return lax.broadcasted_iota(jnp.int32, shape, dim)


def as_bf16(mask):
    return jnp.where(mask, 1.0, 0.0).astype(BF16)


def copy_to(src, dst, send_sem, recv_sem, device):
    return pltpu.make_async_remote_copy(
        src_ref=src,
        dst_ref=dst,
        send_sem=send_sem,
        recv_sem=recv_sem,
        device_id=device,
        device_id_type=MESH,
    )


def kernel(
    side,
    heads,
    grad_ref,
    input_ref,
    w_ref,
    q_ref,
    k_ref,
    v_ref,
    cid_ref,
    dq_ref,
    dk_ref,
    dv_ref,
    wg_ref,
    grad_land,
    input_land,
    pick,
    unpick,
    packed,
    send1,
    land1,
    land2,
    back1,
    land3,
    land4,
    turned,
    turned_land,
    low_grads,
    part_send,
    part_land,
    part_sum,
    last_land,
    x_send,
    x_recv,
    i_send,
    i_recv,
    s1_send,
    s1_recv,
    s2_send,
    s2_recv,
    b1_send,
    b1_recv,
    b2_send,
    b2_recv,
    t_send,
    t_recv,
    g_send,
    g_recv,
    p_send,
    p_recv,
    l_send,
    l_recv,
):
    n = side
    shift = n.bit_length() - 1
    tokens = grad_ref.shape[0]
    cols = grad_ref.shape[1]
    head_dim = w_ref.shape[0]
    clusters = n * n
    rows = clusters * MESSAGE
    scale = 1.0 / math.sqrt(head_dim)

    seq = lax.axis_index("seq")
    mp = lax.axis_index("mp")
    core = seq % 2
    y = seq // 2 // n
    z = seq // 2 % n
    a = y + core * (z - y)
    b = z + core * (y - z)

    def device(first, second, which):
        py = first + which * (second - first)
        pz = second + which * (first - second)
        return ((py * n + pz) * 2 + which, mp)

    def loop(low, high, body):
        def step(i, carry):
            body(i)
            return carry

        lax.fori_loop(low, high, step, 0)

    barrier = pltpu.get_barrier_semaphore()

    def greet(to):
        pl.semaphore_signal(barrier, inc=1, device_id=to, device_id_type=MESH)

    def greet_lines(i):
        there_y = (y + i) % n
        there_z = (z + i) % n
        for which in range(2):
            greet(((there_y * n + z) * 2 + which, mp))
            greet(((y * n + there_z) * 2 + which, mp))

    loop(1, n, greet_lines)
    greet((seq + 1 - 2 * core, mp))
    for off in range(1, heads):
        greet((seq, (mp + off) % heads))

    cid = cid_ref[0]
    along = jnp.broadcast_to(cid, (tokens, tokens))
    at_row = iota((tokens, tokens), 0)
    at_col = iota((tokens, tokens), 1)
    cid_row = jnp.sum(jnp.where(at_row == at_col, along, 0), axis=0, keepdims=True)
    same = along == cid_row
    slot_row = jnp.sum(jnp.where(same & (at_row < at_col), 1, 0), axis=0, keepdims=True)
    slot_col = jnp.sum(jnp.where(same & (at_col < at_row), 1, 0), axis=1, keepdims=True)
    step_a = n - core * (n - 1)
    step_b = 1 + core * (n - 1)

    def token_key(r):
        group = lax.shift_right_logical(r, 3)
        first = lax.shift_right_logical(group, shift)
        second = group & (n - 1)
        return (first * step_a + second * step_b) * 2 + (r & 1)

    target_row = cid_row * 2 + slot_row
    target_col = cid * 2 + slot_col
    r_col = iota((rows, 1), 0)
    r_row = iota((1, rows), 1)
    key_col = token_key(r_col)
    key_row = token_key(r_row)
    kind_col = lax.shift_right_logical(r_col, 1) & 3
    kind_row = lax.shift_right_logical(r_row, 1) & 3
    total = None
    for kind, ref in enumerate((q_ref, k_ref, v_ref)):
        chosen = as_bf16(jnp.where(kind_col == kind, key_col, -1) == target_row)
        term = dot(chosen, ref[0])
        total = term if total is None else total + term
        unpick[kind] = as_bf16(jnp.where(kind_row == kind, key_row, -1) == target_col)
    packed[...] = total
    pick[...] = as_bf16(jnp.where(kind_col == 3, key_col, -1) == target_row)

    partners = (2 * n - 1) + 2 * (n - 1) + heads - 1
    pl.semaphore_wait(barrier, partners)

    def x_copy(src, land, sends, recvs, off):
        return copy_to(
            src, land.at[off - 1], sends.at[off - 1], recvs.at[off - 1], (seq, (mp + off) % heads)
        )

    for off in range(1, heads):
        x_copy(grad_ref, grad_land, x_send, x_recv, off).start()

    def w_part(owner):
        return w_ref[:, pl.ds(pl.multiple_of(owner * cols, cols), cols)]

    head_grad = dot(grad_ref[...], w_part(mp), NT)
    for off in range(1, heads):
        x_copy(grad_ref, grad_land, x_send, x_recv, off).wait_recv()
        head_grad += dot(grad_land[off - 1], w_part((mp + heads - off) % heads), NT)
    for off in range(1, heads):
        x_copy(input_ref, input_land, i_send, i_recv, off).start()
    filled = packed[...] + dot(pick[...], head_grad.astype(BF16))
    send1[...] = filled.reshape(clusters, MESSAGE, head_dim).astype(BF16)

    def first_copy(off, to, source):
        return copy_to(
            send1.at[pl.ds(to * n, n)],
            land1.at[source],
            s1_send.at[off],
            s1_recv.at[off],
            device(to, b, core),
        )

    loop(1, n, lambda i: first_copy(i, (a + i) % n, a).start())
    land1[a] = send1[pl.ds(a * n, n)]
    loop(1, n, lambda i: first_copy(i, a, (a + n - i) % n).wait_recv())

    def second_copy(off, to, which, source):
        return copy_to(
            land1.at[:, to],
            land2.at[which, source],
            s2_send.at[off],
            s2_recv.at[which, off],
            ((lambda d: (d[0] - which, mp))(device(a, to, which))),
        )

    @pl.when(core == 0)
    def _():
        loop(1, n, lambda i: second_copy(i, (b + i) % n, 0, b).start())
        land2[0, b] = land1[:, b]

    @pl.when(core == 1)
    def _():
        loop(0, n, lambda i: second_copy(i, (b + i) % n, 1, b).start())

    count = 2 * clusters * MOST
    lot = min(256, 2 * rows)
    part = lot // KINDS
    lots = 2 * rows // lot

    def place(p):
        which = p // (2 * clusters)
        second = p // (2 * n) % n
        first = p // 2 % n
        py = first + which * (second - first)
        pz = second + which * (first - second)
        return ((py * n + pz) * 2 + which) * 2 + p % 2

    def back_copy(off, to, which, source):
        relay = (y * n + to) * 2 if which == 0 else (to * n + z) * 2 + 1
        return copy_to(
            back1.at[which, to],
            land3.at[source],
            b1_send.at[which, off],
            b1_recv.at[off],
            (relay, mp),
        )

    @pl.when(core == 0)
    def _():
        out_row = iota((lot, lot), 0)
        in_row = iota((lot, lot), 1)
        out_at = out_row % part
        wanted = (out_at // 2) * MESSAGE + (out_row // part) * 2 + out_at % 2
        split = as_bf16(wanted == in_row)
        out_row = iota((lot, 3 * part), 0)
        in_row = iota((lot, 3 * part), 1)
        wanted = (out_row // 2 % 4) * part + (out_row // MESSAGE) * 2 + out_row % 2
        join = as_bf16(wanted == in_row)
        allowed = place(iota((count, 1), 0)) <= place(iota((1, count), 1))

        loop(1, n, lambda i: second_copy(i, b, 0, (b + n - i) % n).wait_recv())
        loop(
            0,
            n,
            lambda i: copy_to(
                land1.at[:, 0],
                land2.at[1, (y + n - i) % n],
                s2_send.at[0],
                s2_recv.at[1, i],
                (seq + 1, mp),
            ).wait_recv(),
        )
        got = land2[...].astype(F32).reshape(2 * rows, head_dim).astype(BF16)
        pieces = [[] for _ in range(KINDS)]
        for i in range(lots):
            parted = dot(split, got[i * lot : (i + 1) * lot]).astype(BF16)
            for kind in range(KINDS):
                pieces[kind].append(parted[kind * part : (kind + 1) * part])
        queries, keys, values, grads = (jnp.concatenate(p, axis=0) for p in pieces)
        scores = jnp.where(allowed, dot(keys, queries, NT) * scale, -1e30)
        weights = jnp.exp(scores - jnp.max(scores, axis=0, keepdims=True))
        probs = weights / jnp.sum(weights, axis=0, keepdims=True)
        probs_low = probs.astype(BF16)
        prob_grad = dot(values, grads, NT)
        delta = jnp.sum(probs_low.astype(F32) * prob_grad, axis=0, keepdims=True)
        dscore = (probs * (prob_grad - delta)).astype(BF16)
        value_part = dot(probs_low, grads).astype(BF16)
        key_part = (dot(dscore, queries) * scale).astype(BF16)
        query_part = (dot(dscore, keys, TN) * scale).astype(BF16)
        per = lot // MESSAGE
        outs = []
        for i in range(lots):
            span = slice(i * part, (i + 1) * part)
            three = jnp.concatenate([query_part[span], key_part[span], value_part[span]], axis=0)
            outs.append(dot(join, three))
        whole = jnp.concatenate(outs, axis=0)
        back1[...] = whole.reshape(2, n, n, MESSAGE, head_dim).astype(BF16)
        loop(1, n, lambda i: back_copy(i, (z + i) % n, 0, z).start())
        loop(0, n, lambda i: back_copy(i, (y + i) % n, 1, y).start())
        land3[b] = back1[0, b]
        loop(1, n, lambda i: back_copy(i, z, 0, (z + n - i) % n).wait_recv())

    @pl.when(core == 1)
    def _():
        loop(
            0,
            n,
            lambda i: copy_to(
                back1.at[1, 0],
                land3.at[(b + n - i) % n],
                b1_send.at[1, 0],
                b1_recv.at[i],
                (seq - 1, mp),
            ).wait_recv(),
        )

    def home_copy(off, to, source):
        return copy_to(
            land3.at[:, to],
            land4.at[source],
            b2_send.at[off],
            b2_recv.at[off],
            device(to, b, core),
        )

    loop(1, n, lambda i: home_copy(i, (a + i) % n, a).start())
    land4[a] = land3[:, a]

    for off in range(1, heads):
        x_copy(input_ref, input_land, i_send, i_recv, off).wait_recv()
    wide = 2 * FEATS * n
    out_row = iota((wide, wide), 0)
    in_row = iota((wide, wide), 1)
    half = wide // 2
    out_at = out_row % half
    wanted = (out_at // FEATS) * 2 * FEATS + (out_row // half) * FEATS + out_at % FEATS
    order = as_bf16(wanted == in_row)
    per_block = cols // wide

    def turn(block, index):
        for i in range(per_block):
            py = index * per_block + i
            done = dot(order, block[:, i * wide : (i + 1) * wide], NT).astype(BF16)
            turned[0, py] = done[0:half].reshape(n, FEATS, tokens)
            turned[1, :, py] = done[half:].reshape(n, FEATS, tokens)

    turn(input_ref[...], mp)
    for off in range(1, heads):
        turn(input_land[off - 1], (mp + heads - off) % heads)
    other = seq + 1 - 2 * core
    turn_copy = copy_to(
        turned.at[1 - core], turned_land, t_send.at[0], t_recv.at[0], (other, mp)
    )
    turn_copy.start()

    loop(1, n, lambda i: home_copy(i, a, (a + n - i) % n).wait_recv())
    home = land4[...].astype(F32).reshape(rows, head_dim).astype(BF16)
    for kind, ref in enumerate((dq_ref, dk_ref, dv_ref)):
        value = dot(unpick[kind], home).astype(BF16)
        ref[0] = value
        low_grads[core, :, kind * head_dim : (kind + 1) * head_dim] = value
    share = copy_to(
        low_grads.at[core], low_grads.at[core], g_send.at[0], g_recv.at[0], (other, mp)
    )
    share.start()
    turn_copy.wait_recv()
    copy_to(
        low_grads.at[core], low_grads.at[1 - core], g_send.at[0], g_recv.at[0], (other, mp)
    ).wait_recv()

    both = jnp.concatenate([low_grads[core], low_grads[1 - core]], axis=0)

    def partial(to):
        mine = turned[core, to].reshape(half, tokens)
        theirs = turned_land[to].reshape(half, tokens)
        return dot(jnp.concatenate([mine, theirs], axis=1), both)

    def part_copy(off, to, source):
        return copy_to(
            part_send.at[to],
            part_land.at[source],
            p_send.at[off],
            p_recv.at[off],
            device(to, b, core),
        )

    def send_part(i):
        off = (i + n // 2 - 1) % (n - 1) + 1
        to = (a + off) % n
        part_send[to] = partial(to).astype(BF16)
        part_copy(off, to, a).start()

    loop(0, n - 1, send_part)
    part_sum[...] = partial(a).reshape(part_sum.shape)

    def add_part(i):
        source = (a + n - i) % n
        part_copy(i, a, source).wait_recv()
        part_sum[...] += part_land[source].astype(F32).reshape(part_sum.shape)

    loop(1, n, add_part)

    def last_copy(off, to, source):
        return copy_to(
            part_sum.at[to], last_land.at[source], l_send.at[off], l_recv.at[off], device(a, to, core)
        )

    loop(1, n, lambda i: last_copy(i, (b + i) % n, b).start())
    wg_ref[...] = part_sum[b]

    def add_last(i):
        source = (b + n - i) % n
        last_copy(i, b, source).wait_recv()
        wg_ref[...] += last_land[source]

    loop(1, n, add_last)

    for off in range(1, heads):
        x_copy(grad_ref, grad_land, x_send, x_recv, off).wait_send()
        x_copy(input_ref, input_land, i_send, i_recv, off).wait_send()
    turn_copy.wait_send()
    share.wait_send()

    def all_sent(i):
        first_copy(i, (a + i) % n, a).wait_send()
        home_copy(i, (a + i) % n, a).wait_send()
        part_copy(i, (a + i) % n, a).wait_send()
        last_copy(i, (b + i) % n, b).wait_send()

    loop(1, n, all_sent)

    @pl.when(core == 0)
    def _():
        loop(1, n, lambda i: second_copy(i, (b + i) % n, 0, b).wait_send())
        loop(1, n, lambda i: back_copy(i, (z + i) % n, 0, z).wait_send())
        loop(0, n, lambda i: back_copy(i, (y + i) % n, 1, y).wait_send())

    @pl.when(core == 1)
    def _():
        loop(0, n, lambda i: second_copy(i, (b + i) % n, 1, b).wait_send())


def on_device(layer_input, output_grad, w_out, query_heads, key_heads, value_heads, cluster_ids):
    devices = lax.axis_size("seq")
    heads = lax.axis_size("mp")
    n = math.isqrt(devices // 2)
    tokens, cols = layer_input.shape
    head_dim = query_heads.shape[2]
    clusters = n * n
    rows = clusters * MESSAGE
    half = FEATS * n
    width = 3 * head_dim
    vmem = pl.BlockSpec(memory_space=pltpu.VMEM)
    dma = pltpu.SemaphoreType.DMA
    grad_shape = jax.ShapeDtypeStruct((1, tokens, head_dim), BF16)
    return pl.pallas_call(
        lambda *refs: kernel(n, heads, *refs),
        out_shape=(
            grad_shape,
            grad_shape,
            grad_shape,
            jax.ShapeDtypeStruct((FEATS, width), F32),
        ),
        in_specs=[vmem] * 7,
        out_specs=(vmem,) * 4,
        scratch_shapes=[
            pltpu.VMEM((heads - 1, tokens, cols), BF16),
            pltpu.VMEM((heads - 1, tokens, cols), BF16),
            pltpu.VMEM((rows, tokens), BF16),
            pltpu.VMEM((3, tokens, rows), BF16),
            pltpu.VMEM((rows, head_dim), F32),
            pltpu.VMEM((clusters, MESSAGE, head_dim), BF16),
            pltpu.VMEM((n, n, MESSAGE, head_dim), BF16),
            pltpu.VMEM((2, n, n, MESSAGE, head_dim), BF16),
            pltpu.VMEM((2, n, n, MESSAGE, head_dim), BF16),
            pltpu.VMEM((n, n, MESSAGE, head_dim), BF16),
            pltpu.VMEM((n, n, MESSAGE, head_dim), BF16),
            pltpu.VMEM((2, n, n, FEATS, tokens), BF16),
            pltpu.VMEM((n, n, FEATS, tokens), BF16),
            pltpu.VMEM((2, tokens, width), BF16),
            pltpu.VMEM((n, half, width), BF16),
            pltpu.VMEM((n, half, width), BF16),
            pltpu.VMEM((n, FEATS, width), F32),
            pltpu.VMEM((n, FEATS, width), F32),
            dma((heads - 1,)),
            dma((heads - 1,)),
            dma((heads - 1,)),
            dma((heads - 1,)),
            dma((n,)),
            dma((n,)),
            dma((n,)),
            dma((2, n)),
            dma((2, n)),
            dma((n,)),
            dma((n,)),
            dma((n,)),
            dma((1,)),
            dma((1,)),
            dma((1,)),
            dma((1,)),
            dma((n,)),
            dma((n,)),
            dma((n,)),
            dma((n,)),
        ],
        compiler_params=pltpu.CompilerParams(
            collective_id=0, has_side_effects=True, vmem_limit_bytes=32 * 1024 * 1024
        ),
    )(output_grad, layer_input, w_out, query_heads, key_heads, value_heads, cluster_ids)


def solution(mesh):
    return jax.shard_map(
        on_device,
        mesh=mesh,
        in_specs=(
            P("seq", "mp"),
            P("seq", "mp"),
            P("mp", None),
            P("mp", "seq", None),
            P("mp", "seq", None),
            P("mp", "seq", None),
            P("mp", "seq", None),
        ),
        out_specs=(
            P("mp", "seq", None),
            P("mp", "seq", None),
            P("mp", "seq", None),
            P("seq", "mp"),
        ),
        check_vma=False,
    )
```

```python
import math

import jax
import jax.numpy as jnp
from jax import lax
from jax.experimental import pallas as pl
from jax.experimental.pallas import tpu as pltpu
from jax.sharding import PartitionSpec as P

MOST = 2
KINDS = 4
MESSAGE = MOST * KINDS
FEATS = 16
MESH = pl.DeviceIdType.MESH
F32 = jnp.float32
BF16 = jnp.bfloat16
NT = (((1,), (1,)), ((), ()))
TN = (((0,), (0,)), ((), ()))


def dot(left, right, dims=(((1,), (0,)), ((), ()))):
    return lax.dot_general(left, right, dims, preferred_element_type=F32)


def iota(shape, dim):
    return lax.broadcasted_iota(jnp.int32, shape, dim)


def as_bf16(mask):
    return jnp.where(mask, 1.0, 0.0).astype(BF16)


def copy_to(src, dst, send_sem, recv_sem, device):
    return pltpu.make_async_remote_copy(
        src_ref=src,
        dst_ref=dst,
        send_sem=send_sem,
        recv_sem=recv_sem,
        device_id=device,
        device_id_type=MESH,
    )


def loop(low, high, body):
    def step(i, carry):
        body(i)
        return carry

    lax.fori_loop(low, high, step, 0)


def take(ref, sem):
    pltpu.make_async_copy(ref, ref, sem).wait()


def slots(cid_row):
    tokens = cid_row.shape[1]
    across = jnp.broadcast_to(cid_row, (tokens, tokens))
    at_row = iota((tokens, tokens), 0)
    at_col = iota((tokens, tokens), 1)
    cid_col = jnp.sum(jnp.where(at_row == at_col, across, 0), axis=1, keepdims=True)
    same = across == cid_col
    slot_row = jnp.sum(jnp.where(same & (at_row < at_col), 1, 0), axis=0, keepdims=True)
    slot_col = jnp.sum(jnp.where(same & (at_col < at_row), 1, 0), axis=1, keepdims=True)
    return slot_row, cid_col, slot_col


def kernel(
    side,
    heads,
    grad_hbm,
    input_hbm,
    w_hbm,
    q_hbm,
    k_hbm,
    v_hbm,
    cid_hbm,
    grads_out,
    wg_out,
    grad_ref,
    input_ref,
    w_ref,
    qkv_ref,
    cid_ref,
    in_sem,
    out_sem,
    ready,
    grad_land,
    pick,
    unpick,
    packed,
    send1,
    land2,
    back1,
    home,
    piece0,
    piece1,
    turned,
    low_grads,
    part_send,
    part_land,
    part_sum,
    last_land,
    wg_ref,
    c_send,
    c_recv,
    x_send,
    x_recv,
    i_send,
    i_recv,
    s_send,
    s_recv,
    b_send,
    b_recv,
    h_send,
    h_recv,
    p_send,
    p_recv,
    l_send,
    l_recv,
):
    n = side
    tokens, cols = grad_ref.shape
    head_dim = w_ref.shape[0]
    clusters = n * n
    rows = clusters * MESSAGE
    scale = 1.0 / math.sqrt(head_dim)
    seq = lax.axis_index("seq")
    mp = lax.axis_index("mp")
    core = lax.rem(seq, 2)
    chip = seq // 2
    y = chip // n
    z = lax.rem(chip, n)
    other = seq + 1 - 2 * core
    a = y + core * (z - y)
    b = z + core * (y - z)

    def device(first, second):
        py = first + core * (second - first)
        pz = second + core * (first - second)
        return ((py * n + pz) * 2 + core, mp)

    def far_first(i):
        block = i // (clusters // 4)
        at = lax.rem(i, clusters // 4)

        def far(k):
            return lax.rem(n // 2 + n + (1 - 2 * lax.rem(k, 2)) * ((k + 1) // 2), n)

        dy = far(at // (n // 2) + (n // 2) * (block // 2))
        dz = far(lax.rem(at, n // 2) + (n // 2) * lax.rem(block, 2))
        return lax.rem(y + dy, n) * n + lax.rem(z + dz, n)

    sent = []

    barrier = pltpu.get_barrier_semaphore()

    def greet(to):
        pl.semaphore_signal(barrier, inc=1, device_id=to, device_id_type=MESH)

    def greet_lines(i):
        there_y = lax.rem(y + i, n)
        there_z = lax.rem(z + i, n)
        greet(((there_y * n + z) * 2 + core, mp))
        greet(((y * n + there_z) * 2 + core, mp))
        greet(((y * n + there_z) * 2 + 1 - core, mp))

    for off in range(1, heads):
        greet((seq, lax.rem(mp + off, heads)))
        greet((other, lax.rem(mp + off, heads)))
    greet((other, mp))
    loop(1, n, greet_lines)
    fetches = [
        pltpu.make_async_copy(src, dst, in_sem.at[i])
        for i, (src, dst) in enumerate(
            (
                (grad_hbm, grad_ref),
                (w_hbm, w_ref),
                (cid_hbm, cid_ref.at[core]),
                (q_hbm, qkv_ref.at[pl.ds(0, 1)]),
                (k_hbm, qkv_ref.at[pl.ds(1, 1)]),
                (v_hbm, qkv_ref.at[pl.ds(2, 1)]),
                (input_hbm, input_ref),
            )
        )
    ]
    for fetch in fetches:
        fetch.start()
    pl.semaphore_wait(barrier, 3 * (n - 1) + 1 + 2 * (heads - 1))

    def grad_copy(off):
        return copy_to(
            grad_hbm,
            grad_land.at[off - 1],
            x_send.at[off - 1],
            x_recv.at[off - 1],
            (seq, lax.rem(mp + off, heads)),
        )

    for off in range(1, heads):
        grad_copy(off).start()
        sent.append(grad_copy(off).wait_send)
    loop(
        1,
        n,
        lambda i: pl.semaphore_signal(
            ready,
            inc=1,
            device_id=((lax.rem(y + i, n) * n + z) * 2 + core, mp),
            device_id_type=MESH,
        ),
    )
    fetches[2].wait()
    cid_copy = copy_to(
        cid_ref.at[core], cid_ref.at[core], c_send.at[0], c_recv.at[0], (other, mp)
    )
    cid_copy.start()
    sent.append(cid_copy.wait_send)

    cid_row = cid_ref[core]
    slot_row = slots(cid_row)[0]
    target_row = cid_row * MOST + slot_row
    r_col = iota((rows, 1), 0)
    key_col = (r_col // MESSAGE) * MOST + r_col % MOST
    kind_col = r_col // MOST % KINDS
    for i in range(3, 6):
        fetches[i].wait()
    total = None
    for kind in range(3):
        chosen = as_bf16(jnp.where(kind_col == kind, key_col, -1) == target_row)
        term = dot(chosen, qkv_ref[kind])
        total = term if total is None else total + term
    packed[...] = total
    pick[...] = as_bf16(jnp.where(kind_col == 3, key_col, -1) == target_row)

    fetches[6].wait()
    wide = 2 * FEATS * n
    half = wide // 2
    out_row = iota((wide, wide), 0)
    in_row = iota((wide, wide), 1)
    out_at = out_row % half
    wanted = (out_at // FEATS) * 2 * FEATS + (out_row // half) * FEATS + out_at % FEATS
    order = as_bf16(wanted == in_row)
    blocks = cols // wide
    for i in range(blocks):
        done = dot(order, input_ref[:, i * wide : (i + 1) * wide], NT).astype(BF16)
        piece0[i] = done[0:half].reshape(n, FEATS, tokens)
        piece1[:, i] = done[half:].reshape(n, FEATS, tokens)

    take(cid_ref.at[0], c_recv.at[0])
    home_rows = 2 * rows
    r_row = iota((1, home_rows), 1)
    spot = r_row // (2 * MESSAGE)
    which = spot // (clusters // 2)
    from_cluster = (spot - which * (clusters // 2)) * 2 + which
    key_row = (from_cluster * 2 + r_row // MESSAGE % 2) * MOST + r_row % MOST
    kind_row = r_row // MOST % KINDS
    for of in range(2):
        _, cid_col, slot_col = slots(cid_ref[of])
        wanted = (cid_col * 2 + of) * MOST + slot_col
        for kind in range(3):
            at = (of * 3 + kind) * tokens
            unpick[at : at + tokens] = as_bf16(
                jnp.where(kind_row == kind, key_row, -1) == wanted
            )

    def w_part(owner):
        return w_ref[:, pl.ds(pl.multiple_of(owner * cols, cols), cols)]

    fetches[0].wait()
    fetches[1].wait()
    head_grad = dot(grad_ref[...], w_part(mp), NT)
    for off in range(1, heads):
        grad_copy(off).wait_recv()
        head_grad += dot(grad_land[off - 1], w_part(lax.rem(mp + heads - off, heads)), NT)
    filled = packed[...] + dot(pick[...], head_grad.astype(BF16))
    send1[...] = filled.reshape(clusters, MESSAGE, head_dim).astype(BF16)
    pl.semaphore_wait(ready, n - 1)

    def to_owner(i):
        to = far_first(i)
        copy_to(
            send1.at[to], land2.at[seq], s_send.at[0], s_recv.at[0], (to * 2, mp)
        ).start()

    loop(0, clusters - 1 + core, to_owner)

    @pl.when(core == 0)
    def _():
        land2[seq] = send1[chip]

    def owner_sent():
        @pl.when(core == 0)
        def _():
            take(send1.at[pl.ds(0, clusters - 1)], s_send.at[0])

        @pl.when(core == 1)
        def _():
            take(send1, s_send.at[0])

    sent.append(owner_sent)

    def input_copy(off, of, to, received=False):
        at = pl.ds(lax.rem(mp + heads - off, heads) * blocks, blocks)
        here = pl.ds(mp * blocks, blocks)
        src, mine, theirs = (
            (piece0, turned.at[of, here], turned.at[of, at])
            if to == 0
            else (piece1, turned.at[of, :, here], turned.at[of, :, at])
        )
        sems = (i_send.at[2 * off + to], i_recv.at[2 * off + of])
        goal = (seq - core + to, lax.rem(mp + off, heads))
        return copy_to(src, theirs if received else mine, *sems, goal)

    def inputs(act):
        for off in range(heads):
            for to in range(2):
                if off == 0:

                    @pl.when(core != to)
                    def _():
                        act(off, to)
                else:
                    act(off, to)

    inputs(lambda off, to: input_copy(off, core, to).start())
    sent.append(lambda: inputs(lambda off, to: input_copy(off, core, to).wait_send()))

    @pl.when(core == 0)
    def _():
        turned[0, pl.ds(mp * blocks, blocks)] = piece0[...]

    @pl.when(core == 1)
    def _():
        turned[1, :, pl.ds(mp * blocks, blocks)] = piece1[...]

    @pl.when(core == 0)
    def _():
        take(land2.at[pl.ds(0, 2 * clusters - 1)], s_recv.at[0])

    count = 2 * clusters * MOST
    lot = min(256, 2 * rows)
    part = lot // KINDS
    lots = 2 * rows // lot

    def to_home(i, to_core):
        to = far_first(i)
        copy_to(
            back1.at[to],
            home.at[to_core, chip // 2],
            b_send.at[0],
            b_recv.at[0],
            (to * 2 + to_core, mp),
        ).start()

    even = lax.rem(chip, 2) == 0

    @pl.when(core == 0)
    def _():
        out_row = iota((lot, lot), 0)
        in_row = iota((lot, lot), 1)
        out_at = out_row % part
        wanted = (out_at // 2) * MESSAGE + (out_row // part) * 2 + out_at % 2
        split = as_bf16(wanted == in_row)
        out_row = iota((lot, 3 * part), 0)
        in_row = iota((lot, 3 * part), 1)
        wanted = (out_row // 2 % 4) * part + (out_row // MESSAGE) * 2 + out_row % 2
        join = as_bf16(wanted == in_row)
        allowed = iota((count, count), 0) <= iota((count, count), 1)
        got = land2[...].astype(F32).reshape(2 * rows, head_dim).astype(BF16)
        pieces = [[] for _ in range(KINDS)]
        for i in range(lots):
            parted = dot(split, got[i * lot : (i + 1) * lot]).astype(BF16)
            for kind in range(KINDS):
                pieces[kind].append(parted[kind * part : (kind + 1) * part])
        queries, keys, values, grads = (jnp.concatenate(p, axis=0) for p in pieces)
        scores = jnp.where(allowed, dot(keys, queries, NT) * scale, -1e30)
        weights = jnp.exp(scores - jnp.max(scores, axis=0, keepdims=True))
        probs = weights / jnp.sum(weights, axis=0, keepdims=True)
        probs_low = probs.astype(BF16)
        prob_grad = dot(values, grads, NT)
        delta = jnp.sum(probs_low.astype(F32) * prob_grad, axis=0, keepdims=True)
        dscore = (probs * (prob_grad - delta)).astype(BF16)
        value_part = dot(probs_low, grads).astype(BF16)
        key_part = (dot(dscore, queries) * scale).astype(BF16)
        query_part = (dot(dscore, keys, TN) * scale).astype(BF16)
        outs = []
        for i in range(lots):
            span = slice(i * part, (i + 1) * part)
            three = jnp.concatenate([query_part[span], key_part[span], value_part[span]], axis=0)
            outs.append(dot(join, three))
        whole = jnp.concatenate(outs, axis=0).astype(BF16)
        back1[...] = whole.reshape(clusters, 2 * MESSAGE, head_dim)

        @pl.when(even)
        def _():
            loop(0, clusters - 1, lambda i: to_home(i, 0))
            home[0, chip // 2] = back1[chip]

        @pl.when(jnp.logical_not(even))
        def _():
            loop(0, clusters, lambda i: to_home(i, 1))

    def back_sent():
        @pl.when((core == 0) & even)
        def _():
            take(back1.at[pl.ds(0, clusters - 1)], b_send.at[0])

        @pl.when((core == 0) & jnp.logical_not(even))
        def _():
            take(back1, b_send.at[0])

    sent.append(back_sent)

    @pl.when((core == 0) & even)
    def _():
        take(home.at[0, pl.ds(0, clusters // 2 - 1)], b_recv.at[0])

    @pl.when((core == 1) | jnp.logical_not(even))
    def _():
        take(home.at[0], b_recv.at[0])

    swap = copy_to(home.at[core], home.at[core], h_send.at[0], h_recv.at[0], (other, mp))
    swap.start()
    sent.append(swap.wait_send)
    take(home.at[0], h_recv.at[0])

    ordered = dot(unpick[...], home[...].reshape(home_rows, head_dim)).astype(BF16)
    for of in range(2):
        for kind in range(3):
            at = (of * 3 + kind) * tokens
            low_grads[of, :, kind * head_dim : (kind + 1) * head_dim] = ordered[at : at + tokens]
    out_copies = [
        pltpu.make_async_copy(
            low_grads.at[core, :, pl.ds(kind * head_dim, head_dim)],
            grads_out.at[kind],
            out_sem.at[kind],
        )
        for kind in range(3)
    ]
    for out_copy in out_copies:
        out_copy.start()
        sent.append(out_copy.wait)
    for mine in range(2):

        @pl.when(core == mine)
        def _():
            for off in range(heads):
                for of in range(2):
                    if off or of != mine:
                        input_copy(off, of, mine, True).wait_recv()

    both = jnp.concatenate([low_grads[0], low_grads[1]], axis=0)

    def partial(to):
        left = [turned[of, to].reshape(half, tokens) for of in range(2)]
        return dot(jnp.concatenate(left, axis=1), both)

    def part_copy(off, to, source):
        return copy_to(
            part_send.at[to], part_land.at[source], p_send.at[off], p_recv.at[off], device(to, b)
        )

    def send_part(i):
        off = lax.rem(i + n // 2 - 1, n - 1) + 1
        to = lax.rem(a + off, n)
        part_send[to] = partial(to).astype(BF16)
        part_copy(off, to, a).start()

    loop(0, n - 1, send_part)
    sent.append(lambda: loop(1, n, lambda i: part_copy(i, lax.rem(a + i, n), a).wait_send()))
    part_sum[...] = partial(a).reshape(part_sum.shape)

    def add_part(i):
        source = lax.rem(a + n - i, n)
        part_copy(i, a, source).wait_recv()
        part_sum[...] += part_land[source].astype(F32).reshape(part_sum.shape)

    loop(1, n, add_part)

    def last_copy(off, to, source):
        return copy_to(
            part_sum.at[to], last_land.at[source], l_send.at[off], l_recv.at[off], device(a, to)
        )

    loop(1, n, lambda i: last_copy(i, lax.rem(b + i, n), b).start())
    sent.append(lambda: loop(1, n, lambda i: last_copy(i, lax.rem(b + i, n), b).wait_send()))
    wg_ref[...] = part_sum[b]

    def add_last(i):
        source = lax.rem(b + n - i, n)
        last_copy(i, b, source).wait_recv()
        wg_ref[...] += last_land[source]

    loop(1, n, add_last)
    wg_copy = pltpu.make_async_copy(wg_ref, wg_out, out_sem.at[3])
    wg_copy.start()
    sent.append(wg_copy.wait)

    for wait_sent in sent:
        wait_sent()


def hand_out(grads_in, wg_in, dq_out, dk_out, dv_out, wg_out):
    for kind, out in enumerate((dq_out, dk_out, dv_out)):
        out[0] = grads_in[kind]
    wg_out[...] = wg_in[...]


def on_device(layer_input, output_grad, w_out, query_heads, key_heads, value_heads, cluster_ids):
    devices = lax.axis_size("seq")
    heads = lax.axis_size("mp")
    n = math.isqrt(devices // 2)
    tokens, cols = layer_input.shape
    head_dim = query_heads.shape[2]
    clusters = n * n
    rows = clusters * MESSAGE
    half = FEATS * n
    blocks = cols // (2 * half)
    width = 3 * head_dim
    hbm = pl.BlockSpec(memory_space=pltpu.HBM)
    dma = pltpu.SemaphoreType.DMA
    grad_shape = jax.ShapeDtypeStruct((1, tokens, head_dim), BF16)
    wg_shape = jax.ShapeDtypeStruct((FEATS, width), F32)
    grads, weight_grad = pl.pallas_call(
        lambda *refs: kernel(n, heads, *refs),
        out_shape=(jax.ShapeDtypeStruct((3, tokens, head_dim), BF16), wg_shape),
        in_specs=[hbm] * 7,
        out_specs=(hbm, hbm),
        scratch_shapes=[
            pltpu.VMEM((tokens, cols), BF16),
            pltpu.VMEM((tokens, cols), BF16),
            pltpu.VMEM((head_dim, heads * cols), BF16),
            pltpu.VMEM((3, tokens, head_dim), BF16),
            pltpu.VMEM((2, 1, tokens), jnp.int32),
            dma((7,)),
            dma((4,)),
            pltpu.SemaphoreType.REGULAR,
            pltpu.VMEM((heads - 1, tokens, cols), BF16),
            pltpu.VMEM((rows, tokens), BF16),
            pltpu.VMEM((6 * tokens, 2 * rows), BF16),
            pltpu.VMEM((rows, head_dim), F32),
            pltpu.VMEM((clusters, MESSAGE, head_dim), BF16),
            pltpu.VMEM((2 * clusters, MESSAGE, head_dim), BF16),
            pltpu.VMEM((clusters, 2 * MESSAGE, head_dim), BF16),
            pltpu.VMEM((2, clusters // 2, 2 * MESSAGE, head_dim), BF16),
            pltpu.VMEM((blocks, n, FEATS, tokens), BF16),
            pltpu.VMEM((n, blocks, FEATS, tokens), BF16),
            pltpu.VMEM((2, n, n, FEATS, tokens), BF16),
            pltpu.VMEM((2, tokens, width), BF16),
            pltpu.VMEM((n, half, width), BF16),
            pltpu.VMEM((n, half, width), BF16),
            pltpu.VMEM((n, FEATS, width), F32),
            pltpu.VMEM((n, FEATS, width), F32),
            pltpu.VMEM((FEATS, width), F32),
            dma((1,)),
            dma((1,)),
            dma((heads - 1,)),
            dma((heads - 1,)),
            dma((2 * heads,)),
            dma((2 * heads,)),
            dma((1,)),
            dma((1,)),
            dma((1,)),
            dma((1,)),
            dma((1,)),
            dma((1,)),
            dma((n,)),
            dma((n,)),
            dma((n,)),
            dma((n,)),
        ],
        compiler_params=pltpu.CompilerParams(
            collective_id=0, has_side_effects=True, vmem_limit_bytes=64 * 1024 * 1024
        ),
    )(
        output_grad,
        layer_input,
        w_out,
        query_heads,
        key_heads,
        value_heads,
        cluster_ids.reshape(1, tokens),
    )
    return pl.pallas_call(
        hand_out,
        out_shape=(grad_shape, grad_shape, grad_shape, wg_shape),
        in_specs=[pl.BlockSpec(memory_space=pltpu.VMEM)] * 2,
        out_specs=(pl.BlockSpec(memory_space=pltpu.VMEM),) * 4,
        compiler_params=pltpu.CompilerParams(vmem_limit_bytes=64 * 1024 * 1024),
    )(grads, weight_grad)


def solution(mesh):
    return jax.shard_map(
        on_device,
        mesh=mesh,
        in_specs=(
            P("seq", "mp"),
            P("seq", "mp"),
            P("mp", None),
            P("mp", "seq", None),
            P("mp", "seq", None),
            P("mp", "seq", None),
            P("mp", "seq", None),
        ),
        out_specs=(
            P("mp", "seq", None),
            P("mp", "seq", None),
            P("mp", "seq", None),
            P("seq", "mp"),
        ),
        check_vma=False,
    )
```

```python
import math

import jax
import jax.numpy as jnp
from jax import lax
from jax.experimental import pallas as pl
from jax.experimental.pallas import tpu as pltpu
from jax.sharding import PartitionSpec as P

MOST = 2
KINDS = 4
MESSAGE = MOST * KINDS
FEATS = 16
MESH = pl.DeviceIdType.MESH
F32 = jnp.float32
BF16 = jnp.bfloat16
NT = (((1,), (1,)), ((), ()))
TN = (((0,), (0,)), ((), ()))


def dot(left, right, dims=(((1,), (0,)), ((), ()))):
    return lax.dot_general(left, right, dims, preferred_element_type=F32)


def iota(shape, dim):
    return lax.broadcasted_iota(jnp.int32, shape, dim)


def as_bf16(mask):
    return jnp.where(mask, 1.0, 0.0).astype(BF16)


def copy_to(src, dst, send_sem, recv_sem, device):
    return pltpu.make_async_remote_copy(
        src_ref=src,
        dst_ref=dst,
        send_sem=send_sem,
        recv_sem=recv_sem,
        device_id=device,
        device_id_type=MESH,
    )


def take(ref, sem):
    pltpu.make_async_copy(ref, ref, sem).wait()


def slots(cid_row):
    tokens = cid_row.shape[1]
    across = jnp.broadcast_to(cid_row, (tokens, tokens))
    at_row = iota((tokens, tokens), 0)
    at_col = iota((tokens, tokens), 1)
    cid_col = jnp.sum(jnp.where(at_row == at_col, across, 0), axis=1, keepdims=True)
    same = across == cid_col
    slot_row = jnp.sum(jnp.where(same & (at_row < at_col), 1, 0), axis=0, keepdims=True)
    slot_col = jnp.sum(jnp.where(same & (at_col < at_row), 1, 0), axis=1, keepdims=True)
    return slot_row, cid_col, slot_col


def kernel(
    side,
    heads,
    grad_hbm,
    input_hbm,
    w_hbm,
    q_hbm,
    k_hbm,
    v_hbm,
    cid_hbm,
    grads_out,
    wg_out,
    grad_ref,
    input_ref,
    w_ref,
    qkv_ref,
    cid_ref,
    in_sem,
    out_sem,
    ready,
    grad_land,
    pick,
    unpick,
    packed,
    send1,
    land2,
    back1,
    home,
    piece0,
    piece1,
    turned,
    low_grads,
    part_send,
    part_land,
    part_sum,
    last_send,
    last_land,
    wg_ref,
    c_send,
    c_recv,
    x_send,
    x_recv,
    i_send,
    i_recv,
    s_send,
    s_recv,
    b_send,
    b_recv,
    h_send,
    h_recv,
    p_send,
    p_recv,
    l_send,
    l_recv,
):
    n = side
    tokens, cols = grad_ref.shape
    head_dim = w_ref.shape[0]
    clusters = n * n
    rows = clusters * MESSAGE
    scale = 1.0 / math.sqrt(head_dim)
    seq = lax.axis_index("seq")
    mp = lax.axis_index("mp")
    core = lax.rem(seq, 2)
    chip = seq // 2
    y = chip // n
    z = lax.rem(chip, n)
    other = seq + 1 - 2 * core
    a = y + core * (z - y)
    b = z + core * (y - z)

    def device(first, second):
        py = first + core * (second - first)
        pz = second + core * (first - second)
        return ((py * n + pz) * 2 + core, mp)

    ys = [lax.rem(y + d, n) for d in range(n)]
    zs = [lax.rem(z + d, n) for d in range(n)]
    firsts = [ys[d] + core * (zs[d] - ys[d]) for d in range(n)]
    seconds = [zs[d] + core * (ys[d] - zs[d]) for d in range(n)]
    away = sorted(
        ((dy, dz) for dy in range(n) for dz in range(n) if dy or dz),
        key=lambda d: -min(d[0], n - d[0]) - min(d[1], n - d[1]),
    )

    sent = []

    barrier = pltpu.get_barrier_semaphore()

    def greet(to):
        pl.semaphore_signal(barrier, inc=1, device_id=to, device_id_type=MESH)

    for off in range(1, heads):
        greet((seq, lax.rem(mp + off, heads)))
        greet((other, lax.rem(mp + off, heads)))
    greet((other, mp))
    for d in range(1, n):
        greet(((ys[d] * n + z) * 2 + core, mp))
        greet(((y * n + zs[d]) * 2 + core, mp))
        greet(((y * n + zs[d]) * 2 + 1 - core, mp))
    fetches = [
        pltpu.make_async_copy(src, dst, in_sem.at[i])
        for i, (src, dst) in enumerate(
            (
                (grad_hbm, grad_ref),
                (w_hbm, w_ref),
                (cid_hbm, cid_ref.at[core]),
                (q_hbm, qkv_ref.at[pl.ds(0, 1)]),
                (k_hbm, qkv_ref.at[pl.ds(1, 1)]),
                (v_hbm, qkv_ref.at[pl.ds(2, 1)]),
                (input_hbm, input_ref),
            )
        )
    ]
    for fetch in fetches:
        fetch.start()
    pl.semaphore_wait(barrier, 3 * (n - 1) + 1 + 2 * (heads - 1))

    def grad_copy(off):
        return copy_to(
            grad_ref,
            grad_land.at[off - 1],
            x_send.at[off - 1],
            x_recv.at[off - 1],
            (seq, lax.rem(mp + off, heads)),
        )

    fetches[0].wait()
    for off in range(1, heads):
        grad_copy(off).start()
        sent.append(grad_copy(off).wait_send)
    for d in range(1, n):
        pl.semaphore_signal(
            ready, inc=1, device_id=((ys[d] * n + z) * 2 + core, mp), device_id_type=MESH
        )
    fetches[2].wait()
    cid_copy = copy_to(
        cid_ref.at[core], cid_ref.at[core], c_send.at[0], c_recv.at[0], (other, mp)
    )
    cid_copy.start()
    sent.append(cid_copy.wait_send)

    cid_row = cid_ref[core]
    slot_row = slots(cid_row)[0]
    target_row = cid_row * MOST + slot_row
    r_col = iota((rows, 1), 0)
    key_col = (r_col // MESSAGE) * MOST + r_col % MOST
    kind_col = r_col // MOST % KINDS
    for i in range(3, 6):
        fetches[i].wait()
    total = None
    for kind in range(3):
        chosen = as_bf16(jnp.where(kind_col == kind, key_col, -1) == target_row)
        term = dot(chosen, qkv_ref[kind])
        total = term if total is None else total + term
    packed[...] = total
    pick[...] = as_bf16(jnp.where(kind_col == 3, key_col, -1) == target_row)

    def w_part(owner):
        return w_ref[:, pl.ds(pl.multiple_of(owner * cols, cols), cols)]

    fetches[1].wait()
    head_grad = dot(grad_ref[...], w_part(mp), NT)
    for off in range(1, heads):
        grad_copy(off).wait_recv()
        head_grad += dot(grad_land[off - 1], w_part(lax.rem(mp + heads - off, heads)), NT)
    filled = packed[...] + dot(pick[...], head_grad.astype(BF16))
    send1[...] = filled.reshape(clusters, MESSAGE, head_dim).astype(BF16)
    pl.semaphore_wait(ready, n - 1)

    def to_owner(to):
        copy_to(
            send1.at[to], land2.at[seq], s_send.at[0], s_recv.at[0], (to * 2, mp)
        ).start()

    for dy, dz in away:
        to_owner(ys[dy] * n + zs[dz])

    @pl.when(core == 0)
    def _():
        land2[seq] = send1[chip]

    @pl.when(core == 1)
    def _():
        to_owner(chip)

    def owner_sent():
        @pl.when(core == 0)
        def _():
            take(send1.at[pl.ds(0, clusters - 1)], s_send.at[0])

        @pl.when(core == 1)
        def _():
            take(send1, s_send.at[0])

    sent.append(owner_sent)

    fetches[6].wait()
    wide = 2 * FEATS * n
    half = wide // 2
    out_row = iota((wide, wide), 0)
    in_row = iota((wide, wide), 1)
    out_at = out_row % half
    wanted = (out_at // FEATS) * 2 * FEATS + (out_row // half) * FEATS + out_at % FEATS
    order = as_bf16(wanted == in_row)
    blocks = cols // wide
    for i in range(blocks):
        done = dot(order, input_ref[:, i * wide : (i + 1) * wide], NT).astype(BF16)
        piece0[i] = done[0:half].reshape(n, FEATS, tokens)
        piece1[:, i] = done[half:].reshape(n, FEATS, tokens)

    take(cid_ref.at[0], c_recv.at[0])
    r_row = iota((1, rows), 1)
    key_row = (r_row // (2 * MESSAGE) * 4 + r_row // MESSAGE % 2) * MOST + r_row % MOST
    kind_row = r_row // MOST % KINDS
    for of in range(2):
        _, cid_col, slot_col = slots(cid_ref[of])
        wanted = (cid_col * 2 + of) * MOST + slot_col
        for kind in range(3):
            at = (of * 3 + kind) * tokens
            for odd in range(2):
                unpick[odd, at : at + tokens] = as_bf16(
                    jnp.where(kind_row == kind, key_row + 2 * MOST * odd, -1) == wanted
                )

    def input_copy(off, of, to, received=False):
        at = pl.ds(lax.rem(mp + heads - off, heads) * blocks, blocks)
        here = pl.ds(mp * blocks, blocks)
        src, mine, theirs = (
            (piece0, turned.at[of, here], turned.at[of, at])
            if to == 0
            else (piece1, turned.at[of, :, here], turned.at[of, :, at])
        )
        sems = (i_send.at[2 * off + to], i_recv.at[2 * off + of])
        goal = (seq - core + to, lax.rem(mp + off, heads))
        return copy_to(src, theirs if received else mine, *sems, goal)

    def inputs(act):
        for off in range(heads):
            for to in range(2):
                if off == 0:

                    @pl.when(core != to)
                    def _():
                        act(off, to)
                else:
                    act(off, to)

    inputs(lambda off, to: input_copy(off, core, to).start())
    sent.append(lambda: inputs(lambda off, to: input_copy(off, core, to).wait_send()))

    @pl.when(core == 0)
    def _():
        turned[0, pl.ds(mp * blocks, blocks)] = piece0[...]

    @pl.when(core == 1)
    def _():
        turned[1, :, pl.ds(mp * blocks, blocks)] = piece1[...]

    @pl.when(core == 0)
    def _():
        take(land2.at[pl.ds(0, 2 * clusters - 1)], s_recv.at[0])

    count = 2 * clusters * MOST
    lot = min(256, 2 * rows)
    part = lot // KINDS
    lots = 2 * rows // lot

    odd = lax.rem(chip, 2)
    even = odd == 0

    def to_home(to):
        copy_to(
            back1.at[to],
            home.at[odd, chip // 2],
            b_send.at[0],
            b_recv.at[0],
            (to * 2 + odd, mp),
        ).start()

    @pl.when(core == 0)
    def _():
        out_row = iota((lot, lot), 0)
        in_row = iota((lot, lot), 1)
        out_at = out_row % part
        wanted = (out_at // 2) * MESSAGE + (out_row // part) * 2 + out_at % 2
        split = as_bf16(wanted == in_row)
        out_row = iota((lot, 3 * part), 0)
        in_row = iota((lot, 3 * part), 1)
        wanted = (out_row // 2 % 4) * part + (out_row // MESSAGE) * 2 + out_row % 2
        join = as_bf16(wanted == in_row)
        allowed = iota((count, count), 0) <= iota((count, count), 1)
        got = land2[...].astype(F32).reshape(2 * rows, head_dim).astype(BF16)
        pieces = [[] for _ in range(KINDS)]
        for i in range(lots):
            parted = dot(split, got[i * lot : (i + 1) * lot]).astype(BF16)
            for kind in range(KINDS):
                pieces[kind].append(parted[kind * part : (kind + 1) * part])
        queries, keys, values, grads = (jnp.concatenate(p, axis=0) for p in pieces)
        scores = jnp.where(allowed, dot(keys, queries, NT) * scale, -1e30)
        weights = jnp.exp(scores - jnp.max(scores, axis=0, keepdims=True))
        probs = weights / jnp.sum(weights, axis=0, keepdims=True)
        probs_low = probs.astype(BF16)
        prob_grad = dot(values, grads, NT)
        delta = jnp.sum(probs_low.astype(F32) * prob_grad, axis=0, keepdims=True)
        dscore = (probs * (prob_grad - delta)).astype(BF16)
        value_part = dot(probs_low, grads).astype(BF16)
        key_part = (dot(dscore, queries) * scale).astype(BF16)
        query_part = (dot(dscore, keys, TN) * scale).astype(BF16)
        outs = []
        for i in range(lots):
            span = slice(i * part, (i + 1) * part)
            three = jnp.concatenate([query_part[span], key_part[span], value_part[span]], axis=0)
            outs.append(dot(join, three))
        whole = jnp.concatenate(outs, axis=0).astype(BF16)
        back1[...] = whole.reshape(clusters, 2 * MESSAGE, head_dim)

        for dy, dz in away:
            to_home(ys[dy] * n + zs[dz])

        @pl.when(even)
        def _():
            home[0, chip // 2] = back1[chip]

        @pl.when(jnp.logical_not(even))
        def _():
            to_home(chip)

    def back_sent():
        @pl.when((core == 0) & even)
        def _():
            take(back1.at[pl.ds(0, clusters - 1)], b_send.at[0])

        @pl.when((core == 0) & jnp.logical_not(even))
        def _():
            take(back1, b_send.at[0])

    sent.append(back_sent)

    @pl.when((core == 0) & even)
    def _():
        take(home.at[0, pl.ds(0, clusters // 2 - 1)], b_recv.at[0])

    @pl.when((core == 1) | jnp.logical_not(even))
    def _():
        take(home.at[0], b_recv.at[0])

    swap = copy_to(home.at[core], home.at[core], h_send.at[0], h_recv.at[0], (other, mp))
    swap.start()
    sent.append(swap.wait_send)
    first_half = dot(unpick[core], home[core].reshape(rows, head_dim))
    take(home.at[0], h_recv.at[0])

    second_half = dot(unpick[1 - core], home[1 - core].reshape(rows, head_dim))
    ordered = (first_half + second_half).astype(BF16)
    for of in range(2):
        for kind in range(3):
            at = (of * 3 + kind) * tokens
            low_grads[of, :, kind * head_dim : (kind + 1) * head_dim] = ordered[at : at + tokens]
    out_copies = [
        pltpu.make_async_copy(
            low_grads.at[core, :, pl.ds(kind * head_dim, head_dim)],
            grads_out.at[kind],
            out_sem.at[kind],
        )
        for kind in range(3)
    ]
    for out_copy in out_copies:
        out_copy.start()
        sent.append(out_copy.wait)
    for mine in range(2):

        @pl.when(core == mine)
        def _():
            for off in range(heads):
                for of in range(2):
                    if off or of != mine:
                        input_copy(off, of, mine, True).wait_recv()

    both = jnp.concatenate([low_grads[0], low_grads[1]], axis=0)

    def partial(to):
        left = [turned[of, to].reshape(half, tokens) for of in range(2)]
        return dot(jnp.concatenate(left, axis=1), both)

    def part_copy(off, to, source):
        return copy_to(
            part_send.at[to], part_land.at[source], p_send.at[off], p_recv.at[off], device(to, b)
        )

    by_distance = sorted(range(1, n), key=lambda d: -min(d, n - d))
    for d in by_distance:
        part_send[firsts[d]] = partial(firsts[d]).astype(BF16)
        part_copy(d, firsts[d], a).start()
    part_sum[...] = partial(a).reshape(part_sum.shape)

    def all_sent():
        for wait_sent in sent:
            wait_sent()
        sent.clear()

    all_sent()
    for d in reversed(by_distance):
        source = firsts[n - d]
        part_copy(d, a, source).wait_recv()
        part_sum[...] += part_land[source].astype(F32).reshape(part_sum.shape)

    def last_copy(off, to, source):
        return copy_to(
            last_send.at[to], last_land.at[source], l_send.at[off], l_recv.at[off], device(a, to)
        )

    last_send[...] = part_sum[...].astype(BF16)
    for d in by_distance:
        last_copy(d, seconds[d], b).start()
        sent.append(last_copy(d, seconds[d], b).wait_send)
    wg_ref[...] = part_sum[b]
    for d in by_distance:
        part_copy(d, firsts[d], a).wait_send()

    for d in reversed(by_distance):
        source = seconds[n - d]
        last_copy(d, b, source).wait_recv()
        wg_ref[...] += last_land[source].astype(F32)
    wg_copy = pltpu.make_async_copy(wg_ref, wg_out, out_sem.at[3])
    wg_copy.start()
    sent.append(wg_copy.wait)

    all_sent()


def hand_out(grads_in, wg_in, dq_out, dk_out, dv_out, wg_out):
    for kind, out in enumerate((dq_out, dk_out, dv_out)):
        out[0] = grads_in[kind]
    wg_out[...] = wg_in[...]


def on_device(layer_input, output_grad, w_out, query_heads, key_heads, value_heads, cluster_ids):
    devices = lax.axis_size("seq")
    heads = lax.axis_size("mp")
    n = math.isqrt(devices // 2)
    tokens, cols = layer_input.shape
    head_dim = query_heads.shape[2]
    clusters = n * n
    rows = clusters * MESSAGE
    half = FEATS * n
    blocks = cols // (2 * half)
    width = 3 * head_dim
    hbm = pl.BlockSpec(memory_space=pltpu.HBM)
    dma = pltpu.SemaphoreType.DMA
    grad_shape = jax.ShapeDtypeStruct((1, tokens, head_dim), BF16)
    wg_shape = jax.ShapeDtypeStruct((FEATS, width), F32)
    grads, weight_grad = pl.pallas_call(
        lambda *refs: kernel(n, heads, *refs),
        out_shape=(jax.ShapeDtypeStruct((3, tokens, head_dim), BF16), wg_shape),
        in_specs=[hbm] * 7,
        out_specs=(hbm, hbm),
        scratch_shapes=[
            pltpu.VMEM((tokens, cols), BF16),
            pltpu.VMEM((tokens, cols), BF16),
            pltpu.VMEM((head_dim, heads * cols), BF16),
            pltpu.VMEM((3, tokens, head_dim), BF16),
            pltpu.VMEM((2, 1, tokens), jnp.int32),
            dma((7,)),
            dma((4,)),
            pltpu.SemaphoreType.REGULAR,
            pltpu.VMEM((heads - 1, tokens, cols), BF16),
            pltpu.VMEM((rows, tokens), BF16),
            pltpu.VMEM((2, 6 * tokens, rows), BF16),
            pltpu.VMEM((rows, head_dim), F32),
            pltpu.VMEM((clusters, MESSAGE, head_dim), BF16),
            pltpu.VMEM((2 * clusters, MESSAGE, head_dim), BF16),
            pltpu.VMEM((clusters, 2 * MESSAGE, head_dim), BF16),
            pltpu.VMEM((2, clusters // 2, 2 * MESSAGE, head_dim), BF16),
            pltpu.VMEM((blocks, n, FEATS, tokens), BF16),
            pltpu.VMEM((n, blocks, FEATS, tokens), BF16),
            pltpu.VMEM((2, n, n, FEATS, tokens), BF16),
            pltpu.VMEM((2, tokens, width), BF16),
            pltpu.VMEM((n, half, width), BF16),
            pltpu.VMEM((n, half, width), BF16),
            pltpu.VMEM((n, FEATS, width), F32),
            pltpu.VMEM((n, FEATS, width), BF16),
            pltpu.VMEM((n, FEATS, width), BF16),
            pltpu.VMEM((FEATS, width), F32),
            dma((1,)),
            dma((1,)),
            dma((heads - 1,)),
            dma((heads - 1,)),
            dma((2 * heads,)),
            dma((2 * heads,)),
            dma((1,)),
            dma((1,)),
            dma((1,)),
            dma((1,)),
            dma((1,)),
            dma((1,)),
            dma((n,)),
            dma((n,)),
            dma((n,)),
            dma((n,)),
        ],
        compiler_params=pltpu.CompilerParams(
            collective_id=0, has_side_effects=True, vmem_limit_bytes=64 * 1024 * 1024
        ),
    )(
        output_grad,
        layer_input,
        w_out,
        query_heads,
        key_heads,
        value_heads,
        cluster_ids.reshape(1, tokens),
    )
    return pl.pallas_call(
        hand_out,
        out_shape=(grad_shape, grad_shape, grad_shape, wg_shape),
        in_specs=[pl.BlockSpec(memory_space=pltpu.VMEM)] * 2,
        out_specs=(pl.BlockSpec(memory_space=pltpu.VMEM),) * 4,
        compiler_params=pltpu.CompilerParams(vmem_limit_bytes=64 * 1024 * 1024),
    )(grads, weight_grad)


def solution(mesh):
    return jax.shard_map(
        on_device,
        mesh=mesh,
        in_specs=(
            P("seq", "mp"),
            P("seq", "mp"),
            P("mp", None),
            P("mp", "seq", None),
            P("mp", "seq", None),
            P("mp", "seq", None),
            P("mp", "seq", None),
        ),
        out_specs=(
            P("mp", "seq", None),
            P("mp", "seq", None),
            P("mp", "seq", None),
            P("seq", "mp"),
        ),
        check_vma=False,
    )
```

```python
import math

import jax
import jax.numpy as jnp
from jax import lax
from jax.experimental import pallas as pl
from jax.experimental.pallas import tpu as pltpu
from jax.sharding import PartitionSpec as P

MOST = 2
KINDS = 4
MESSAGE = MOST * KINDS
FEATS = 16
MESH = pl.DeviceIdType.MESH
F32 = jnp.float32
BF16 = jnp.bfloat16
NT = (((1,), (1,)), ((), ()))
TN = (((0,), (0,)), ((), ()))


def dot(left, right, dims=(((1,), (0,)), ((), ()))):
    return lax.dot_general(left, right, dims, preferred_element_type=F32)


def iota(shape, dim):
    return lax.broadcasted_iota(jnp.int32, shape, dim)


def as_bf16(mask):
    return jnp.where(mask, 1.0, 0.0).astype(BF16)


def copy_to(src, dst, send_sem, recv_sem, device):
    return pltpu.make_async_remote_copy(
        src_ref=src,
        dst_ref=dst,
        send_sem=send_sem,
        recv_sem=recv_sem,
        device_id=device,
        device_id_type=MESH,
    )


def take(ref, sem):
    pltpu.make_async_copy(ref, ref, sem).wait()


def slots(cid_row):
    tokens = cid_row.shape[1]
    across = jnp.broadcast_to(cid_row, (tokens, tokens))
    at_row = iota((tokens, tokens), 0)
    at_col = iota((tokens, tokens), 1)
    cid_col = jnp.sum(jnp.where(at_row == at_col, across, 0), axis=1, keepdims=True)
    same = across == cid_col
    slot_row = jnp.sum(jnp.where(same & (at_row < at_col), 1, 0), axis=0, keepdims=True)
    slot_col = jnp.sum(jnp.where(same & (at_col < at_row), 1, 0), axis=1, keepdims=True)
    return slot_row, cid_col, slot_col


def kernel(
    side,
    heads,
    grad_hbm,
    input_hbm,
    w_hbm,
    q_hbm,
    k_hbm,
    v_hbm,
    cid_hbm,
    grads_out,
    wg_out,
    grad_ref,
    input_ref,
    w_ref,
    qkv_ref,
    cid_ref,
    in_sem,
    ready,
    grad_land,
    pick,
    unpick,
    packed,
    split_ref,
    join_ref,
    send1,
    land2,
    back1,
    home,
    piece0,
    piece1,
    turned,
    both_ref,
    part_send,
    part_land,
    part_sum,
    last_send,
    last_land,
    c_send,
    c_recv,
    x_send,
    x_recv,
    i_send,
    i_recv,
    s_send,
    s_recv,
    b_send,
    b_recv,
    h_send,
    h_recv,
    p_send,
    p_recv,
    l_send,
    l_recv,
):
    n = side
    tokens, cols = grad_ref.shape
    head_dim = w_ref.shape[0]
    clusters = n * n
    rows = clusters * MESSAGE
    scale = 1.0 / math.sqrt(head_dim)
    seq = lax.axis_index("seq")
    mp = lax.axis_index("mp")
    core = lax.rem(seq, 2)
    chip = seq // 2
    y = chip // n
    z = lax.rem(chip, n)
    other = seq + 1 - 2 * core
    a = y + core * (z - y)
    b = z + core * (y - z)

    def device(first, second):
        py = first + core * (second - first)
        pz = second + core * (first - second)
        return ((py * n + pz) * 2 + core, mp)

    ys = [lax.rem(y + d, n) for d in range(n)]
    zs = [lax.rem(z + d, n) for d in range(n)]
    firsts = [ys[d] + core * (zs[d] - ys[d]) for d in range(n)]
    seconds = [zs[d] + core * (ys[d] - zs[d]) for d in range(n)]
    away = sorted(
        ((dy, dz) for dy in range(n) for dz in range(n) if dy or dz),
        key=lambda d: -min(d[0], n - d[0]) - min(d[1], n - d[1]),
    )

    sent = []

    barrier = pltpu.get_barrier_semaphore()

    def greet(to):
        pl.semaphore_signal(barrier, inc=1, device_id=to, device_id_type=MESH)

    for off in range(1, heads):
        greet((seq, lax.rem(mp + off, heads)))
        greet((other, lax.rem(mp + off, heads)))
    greet((other, mp))
    for d in range(1, n):
        greet(((ys[d] * n + z) * 2 + core, mp))
        greet(((y * n + zs[d]) * 2 + core, mp))
        greet(((y * n + zs[d]) * 2 + 1 - core, mp))
    fetches = [
        pltpu.make_async_copy(src, dst, in_sem.at[i])
        for i, (src, dst) in enumerate(
            (
                (grad_hbm, grad_ref),
                (w_hbm, w_ref),
                (cid_hbm, cid_ref.at[core]),
                (q_hbm, qkv_ref.at[pl.ds(0, 1)]),
                (k_hbm, qkv_ref.at[pl.ds(1, 1)]),
                (v_hbm, qkv_ref.at[pl.ds(2, 1)]),
                (input_hbm, input_ref),
            )
        )
    ]
    for fetch in fetches:
        fetch.start()
    pl.semaphore_wait(barrier, 3 * (n - 1) + 1 + 2 * (heads - 1))

    def grad_copy(off):
        return copy_to(
            grad_ref,
            grad_land.at[off - 1],
            x_send.at[off - 1],
            x_recv.at[off - 1],
            (seq, lax.rem(mp + off, heads)),
        )

    fetches[0].wait()
    for off in range(1, heads):
        grad_copy(off).start()
        sent.append(grad_copy(off).wait_send)
    for d in range(1, n):
        pl.semaphore_signal(
            ready, inc=1, device_id=((ys[d] * n + z) * 2 + core, mp), device_id_type=MESH
        )
    fetches[2].wait()
    cid_copy = copy_to(
        cid_ref.at[core], cid_ref.at[core], c_send.at[0], c_recv.at[0], (other, mp)
    )
    cid_copy.start()
    sent.append(cid_copy.wait_send)

    cid_row = cid_ref[core]
    slot_row = slots(cid_row)[0]
    target_row = cid_row * MOST + slot_row
    r_col = iota((rows, 1), 0)
    key_col = (r_col // MESSAGE) * MOST + r_col % MOST
    kind_col = r_col // MOST % KINDS
    for i in range(3, 6):
        fetches[i].wait()
    total = None
    for kind in range(3):
        chosen = as_bf16(jnp.where(kind_col == kind, key_col, -1) == target_row)
        term = dot(chosen, qkv_ref[kind])
        total = term if total is None else total + term
    packed[...] = total
    pick[...] = as_bf16(jnp.where(kind_col == 3, key_col, -1) == target_row)

    def w_part(owner):
        return w_ref[:, pl.ds(pl.multiple_of(owner * cols, cols), cols)]

    fetches[1].wait()
    head_grad = dot(grad_ref[...], w_part(mp), NT)
    for off in sorted(range(1, heads), key=lambda d: min(d, heads - d)):
        grad_copy(off).wait_recv()
        head_grad += dot(grad_land[off - 1], w_part(lax.rem(mp + heads - off, heads)), NT)
    filled = packed[...] + dot(pick[...], head_grad.astype(BF16))
    send1[...] = filled.reshape(clusters, MESSAGE, head_dim).astype(BF16)
    pl.semaphore_wait(ready, n - 1)

    def to_owner(to):
        copy_to(
            send1.at[to], land2.at[seq], s_send.at[0], s_recv.at[0], (to * 2, mp)
        ).start()

    for dy, dz in away:
        to_owner(ys[dy] * n + zs[dz])

    @pl.when(core == 0)
    def _():
        land2[seq] = send1[chip]

    @pl.when(core == 1)
    def _():
        to_owner(chip)

    def owner_sent():
        @pl.when(core == 0)
        def _():
            take(send1.at[pl.ds(0, clusters - 1)], s_send.at[0])

        @pl.when(core == 1)
        def _():
            take(send1, s_send.at[0])

    sent.append(owner_sent)

    fetches[6].wait()
    wide = 2 * FEATS * n
    half = wide // 2
    out_row = iota((wide, wide), 0)
    in_row = iota((wide, wide), 1)
    out_at = out_row % half
    wanted = (out_at // FEATS) * 2 * FEATS + (out_row // half) * FEATS + out_at % FEATS
    order = as_bf16(wanted == in_row)
    blocks = cols // wide
    for i in range(blocks):
        done = dot(order, input_ref[:, i * wide : (i + 1) * wide], NT).astype(BF16)
        piece0[i] = done[0:half].reshape(n, FEATS, tokens)
        piece1[:, i] = done[half:].reshape(n, FEATS, tokens)

    take(cid_ref.at[0], c_recv.at[0])
    r_row = iota((1, rows), 1)
    key_row = (r_row // (2 * MESSAGE) * 4 + r_row // MESSAGE % 2) * MOST + r_row % MOST
    kind_row = r_row // MOST % KINDS
    for of in range(2):
        _, cid_col, slot_col = slots(cid_ref[of])
        wanted = (cid_col * 2 + of) * MOST + slot_col
        for kind in range(3):
            at = (of * 3 + kind) * tokens
            for odd in range(2):
                unpick[odd, at : at + tokens] = as_bf16(
                    jnp.where(kind_row == kind, key_row + 2 * MOST * odd, -1) == wanted
                )

    def input_copy(off, of, to, received=False):
        at = pl.ds(lax.rem(mp + heads - off, heads) * blocks, blocks)
        here = pl.ds(mp * blocks, blocks)
        src, mine, theirs = (
            (piece0, turned.at[of, here], turned.at[of, at])
            if to == 0
            else (piece1, turned.at[of, :, here], turned.at[of, :, at])
        )
        sems = (i_send.at[2 * off + to], i_recv.at[2 * off + of])
        goal = (seq - core + to, lax.rem(mp + off, heads))
        return copy_to(src, theirs if received else mine, *sems, goal)

    def inputs(act):
        for off in range(heads):
            for to in range(2):
                if off == 0:

                    @pl.when(core != to)
                    def _():
                        act(off, to)
                else:
                    act(off, to)

    inputs(lambda off, to: input_copy(off, core, to).start())
    sent.append(lambda: inputs(lambda off, to: input_copy(off, core, to).wait_send()))

    @pl.when(core == 0)
    def _():
        turned[0, pl.ds(mp * blocks, blocks)] = piece0[...]

    @pl.when(core == 1)
    def _():
        turned[1, :, pl.ds(mp * blocks, blocks)] = piece1[...]

    count = 2 * clusters * MOST
    lot = min(256, 2 * rows)
    part = lot // KINDS
    lots = 2 * rows // lot
    out_row = iota((lot, lot), 0)
    in_row = iota((lot, lot), 1)
    out_at = out_row % part
    wanted = (out_at // 2) * MESSAGE + (out_row // part) * 2 + out_at % 2
    split_ref[...] = as_bf16(wanted == in_row)
    out_row = iota((lot, 3 * part), 0)
    in_row = iota((lot, 3 * part), 1)
    wanted = (out_row // 2 % 4) * part + (out_row // MESSAGE) * 2 + out_row % 2
    join_ref[...] = as_bf16(wanted == in_row)

    @pl.when(core == 0)
    def _():
        take(land2.at[pl.ds(0, 2 * clusters - 1)], s_recv.at[0])


    odd = lax.rem(chip, 2)
    even = odd == 0

    def to_home(to):
        copy_to(
            back1.at[to],
            home.at[odd, chip // 2],
            b_send.at[0],
            b_recv.at[0],
            (to * 2 + odd, mp),
        ).start()

    @pl.when(core == 0)
    def _():
        got = land2[...].astype(F32).reshape(2 * rows, head_dim).astype(BF16)
        pieces = [[] for _ in range(KINDS)]
        for i in range(lots):
            parted = dot(split_ref[...], got[i * lot : (i + 1) * lot]).astype(BF16)
            for kind in range(KINDS):
                pieces[kind].append(parted[kind * part : (kind + 1) * part])
        queries, keys, values, grads = (jnp.concatenate(p, axis=0) for p in pieces)
        allowed = iota((count, count), 0) <= iota((count, count), 1)
        scores = jnp.where(allowed, dot(keys, queries, NT) * scale, -1e30)
        weights = jnp.exp(scores - jnp.max(scores, axis=0, keepdims=True))
        probs = weights / jnp.sum(weights, axis=0, keepdims=True)
        probs_low = probs.astype(BF16)
        prob_grad = dot(values, grads, NT)
        delta = jnp.sum(probs_low.astype(F32) * prob_grad, axis=0, keepdims=True)
        dscore = (probs * (prob_grad - delta)).astype(BF16)
        value_part = dot(probs_low, grads).astype(BF16)
        key_part = (dot(dscore, queries) * scale).astype(BF16)
        query_part = (dot(dscore, keys, TN) * scale).astype(BF16)
        outs = []
        for i in range(lots):
            span = slice(i * part, (i + 1) * part)
            three = jnp.concatenate([query_part[span], key_part[span], value_part[span]], axis=0)
            outs.append(dot(join_ref[...], three))
        whole = jnp.concatenate(outs, axis=0).astype(BF16)
        back1[...] = whole.reshape(clusters, 2 * MESSAGE, head_dim)

        for dy, dz in away:
            to_home(ys[dy] * n + zs[dz])

        @pl.when(even)
        def _():
            home[0, chip // 2] = back1[chip]

        @pl.when(jnp.logical_not(even))
        def _():
            to_home(chip)

    def back_sent():
        @pl.when((core == 0) & even)
        def _():
            take(back1.at[pl.ds(0, clusters - 1)], b_send.at[0])

        @pl.when((core == 0) & jnp.logical_not(even))
        def _():
            take(back1, b_send.at[0])

    sent.append(back_sent)

    @pl.when((core == 0) & even)
    def _():
        take(home.at[0, pl.ds(0, clusters // 2 - 1)], b_recv.at[0])

    @pl.when((core == 1) | jnp.logical_not(even))
    def _():
        take(home.at[0], b_recv.at[0])

    swap = copy_to(home.at[core], home.at[core], h_send.at[0], h_recv.at[0], (other, mp))
    swap.start()
    sent.append(swap.wait_send)
    first_half = dot(unpick[core], home[core].reshape(rows, head_dim))
    take(home.at[0], h_recv.at[0])

    second_half = dot(unpick[1 - core], home[1 - core].reshape(rows, head_dim))
    ordered = (first_half + second_half).astype(BF16)
    for mine in range(2):

        @pl.when(core == mine)
        def _():
            for off in range(heads):
                for of in range(2):
                    if off or of != mine:
                        input_copy(off, of, mine, True).wait_recv()

    halves = [
        jnp.concatenate(
            [ordered[at : at + tokens] for at in range(of * 3 * tokens, (of + 1) * 3 * tokens, tokens)],
            axis=1,
        )
        for of in range(2)
    ]
    both_ref[...] = jnp.concatenate(halves, axis=0)
    both = both_ref[...]

    def partial(to):
        left = [turned[of, to].reshape(half, tokens) for of in range(2)]
        return dot(jnp.concatenate(left, axis=1), both)

    def part_copy(off, to, source):
        return copy_to(
            part_send.at[to], part_land.at[source], p_send.at[off], p_recv.at[off], device(to, b)
        )

    by_distance = sorted(range(1, n), key=lambda d: -min(d, n - d))
    for d in by_distance:
        part_send[firsts[d]] = partial(firsts[d]).astype(BF16)
        part_copy(d, firsts[d], a).start()
    part_sum[...] = partial(a).reshape(part_sum.shape)

    for kind in range(3):
        span = slice(kind * head_dim, (kind + 1) * head_dim)
        grads_out[kind] = both_ref[pl.ds(pl.multiple_of(core * tokens, tokens), tokens), span]

    def all_sent():
        for wait_sent in sent:
            wait_sent()
        sent.clear()

    all_sent()
    for d in reversed(by_distance):
        source = firsts[n - d]
        part_copy(d, a, source).wait_recv()
        part_sum[...] += part_land[source].astype(F32).reshape(part_sum.shape)

    def last_copy(off, to, source):
        return copy_to(
            last_send.at[to], last_land.at[source], l_send.at[off], l_recv.at[off], device(a, to)
        )

    last_send[...] = part_sum[...].astype(BF16)
    for d in by_distance:
        last_copy(d, seconds[d], b).start()
        sent.append(last_copy(d, seconds[d], b).wait_send)
    wg_out[...] = part_sum[b]
    for d in by_distance:
        part_copy(d, firsts[d], a).wait_send()

    for d in reversed(by_distance):
        source = seconds[n - d]
        last_copy(d, b, source).wait_recv()
        wg_out[...] += last_land[source].astype(F32)

    all_sent()


def hand_out(grads_in, wg_in, dq_out, dk_out, dv_out, wg_out, sem):
    copies = [
        pltpu.make_async_copy(grads_in.at[pl.ds(kind, 1)], out, sem.at[kind])
        for kind, out in enumerate((dq_out, dk_out, dv_out))
    ]
    copies.append(pltpu.make_async_copy(wg_in, wg_out, sem.at[3]))
    for copy in copies:
        copy.start()
    for copy in copies:
        copy.wait()


def on_device(layer_input, output_grad, w_out, query_heads, key_heads, value_heads, cluster_ids):
    devices = lax.axis_size("seq")
    heads = lax.axis_size("mp")
    n = math.isqrt(devices // 2)
    tokens, cols = layer_input.shape
    head_dim = query_heads.shape[2]
    clusters = n * n
    rows = clusters * MESSAGE
    half = FEATS * n
    lot = min(256, 2 * rows)
    blocks = cols // (2 * half)
    width = 3 * head_dim
    vmem = pl.BlockSpec(memory_space=pltpu.VMEM)
    hbm = pl.BlockSpec(memory_space=pltpu.HBM)
    dma = pltpu.SemaphoreType.DMA
    grad_shape = jax.ShapeDtypeStruct((1, tokens, head_dim), BF16)
    wg_shape = jax.ShapeDtypeStruct((FEATS, width), F32)
    grads, weight_grad = pl.pallas_call(
        lambda *refs: kernel(n, heads, *refs),
        out_shape=(
            pltpu.VMEM((3, tokens, head_dim), BF16),
            pltpu.VMEM((FEATS, width), F32),
        ),
        in_specs=[hbm] * 7,
        out_specs=(vmem, vmem),
        scratch_shapes=[
            pltpu.VMEM((tokens, cols), BF16),
            pltpu.VMEM((tokens, cols), BF16),
            pltpu.VMEM((head_dim, heads * cols), BF16),
            pltpu.VMEM((3, tokens, head_dim), BF16),
            pltpu.VMEM((2, 1, tokens), jnp.int32),
            dma((7,)),
            pltpu.SemaphoreType.REGULAR,
            pltpu.VMEM((heads - 1, tokens, cols), BF16),
            pltpu.VMEM((rows, tokens), BF16),
            pltpu.VMEM((2, 6 * tokens, rows), BF16),
            pltpu.VMEM((rows, head_dim), F32),
            pltpu.VMEM((lot, lot), BF16),
            pltpu.VMEM((lot, 3 * lot // KINDS), BF16),
            pltpu.VMEM((clusters, MESSAGE, head_dim), BF16),
            pltpu.VMEM((2 * clusters, MESSAGE, head_dim), BF16),
            pltpu.VMEM((clusters, 2 * MESSAGE, head_dim), BF16),
            pltpu.VMEM((2, clusters // 2, 2 * MESSAGE, head_dim), BF16),
            pltpu.VMEM((blocks, n, FEATS, tokens), BF16),
            pltpu.VMEM((n, blocks, FEATS, tokens), BF16),
            pltpu.VMEM((2, n, n, FEATS, tokens), BF16),
            pltpu.VMEM((2 * tokens, width), BF16),
            pltpu.VMEM((n, half, width), BF16),
            pltpu.VMEM((n, half, width), BF16),
            pltpu.VMEM((n, FEATS, width), F32),
            pltpu.VMEM((n, FEATS, width), BF16),
            pltpu.VMEM((n, FEATS, width), BF16),
            dma((1,)),
            dma((1,)),
            dma((heads - 1,)),
            dma((heads - 1,)),
            dma((2 * heads,)),
            dma((2 * heads,)),
            dma((1,)),
            dma((1,)),
            dma((1,)),
            dma((1,)),
            dma((1,)),
            dma((1,)),
            dma((n,)),
            dma((n,)),
            dma((n,)),
            dma((n,)),
        ],
        compiler_params=pltpu.CompilerParams(
            collective_id=0, has_side_effects=True, vmem_limit_bytes=40 * 1024 * 1024
        ),
    )(
        *(
            pltpu.with_memory_space_constraint(x, pltpu.HBM)
            for x in (
                output_grad,
                layer_input,
                w_out,
                query_heads,
                key_heads,
                value_heads,
                cluster_ids.reshape(1, tokens),
            )
        )
    )
    return pl.pallas_call(
        hand_out,
        out_shape=(grad_shape, grad_shape, grad_shape, wg_shape),
        in_specs=[vmem] * 2,
        out_specs=(hbm,) * 4,
        scratch_shapes=[dma((4,))],
        compiler_params=pltpu.CompilerParams(vmem_limit_bytes=16 * 1024 * 1024),
    )(grads, weight_grad)


def solution(mesh):
    return jax.shard_map(
        on_device,
        mesh=mesh,
        in_specs=(
            P("seq", "mp"),
            P("seq", "mp"),
            P("mp", None),
            P("mp", "seq", None),
            P("mp", "seq", None),
            P("mp", "seq", None),
            P("mp", "seq", None),
        ),
        out_specs=(
            P("mp", "seq", None),
            P("mp", "seq", None),
            P("mp", "seq", None),
            P("seq", "mp"),
        ),
        check_vma=False,
    )
```

```python
import math

import jax
import jax.numpy as jnp
from jax import lax
from jax.experimental import pallas as pl
from jax.experimental.pallas import tpu as pltpu
from jax.sharding import PartitionSpec as P

MOST = 2
KINDS = 4
MESSAGE = MOST * KINDS
FEATS = 16
MESH = pl.DeviceIdType.MESH
F32 = jnp.float32
BF16 = jnp.bfloat16
NT = (((1,), (1,)), ((), ()))
TN = (((0,), (0,)), ((), ()))


def dot(left, right, dims=(((1,), (0,)), ((), ()))):
    return lax.dot_general(left, right, dims, preferred_element_type=F32)


def iota(shape, dim):
    return lax.broadcasted_iota(jnp.int32, shape, dim)


def as_bf16(mask):
    return jnp.where(mask, 1.0, 0.0).astype(BF16)


def copy_to(src, dst, send_sem, recv_sem, device):
    return pltpu.make_async_remote_copy(
        src_ref=src,
        dst_ref=dst,
        send_sem=send_sem,
        recv_sem=recv_sem,
        device_id=device,
        device_id_type=MESH,
    )


def take(ref, sem):
    pltpu.make_async_copy(ref, ref, sem).wait()


def slots(cid_row):
    tokens = cid_row.shape[1]
    across = jnp.broadcast_to(cid_row, (tokens, tokens))
    at_row = iota((tokens, tokens), 0)
    at_col = iota((tokens, tokens), 1)
    cid_col = jnp.sum(jnp.where(at_row == at_col, across, 0), axis=1, keepdims=True)
    same = across == cid_col
    slot_row = jnp.sum(jnp.where(same & (at_row < at_col), 1, 0), axis=0, keepdims=True)
    slot_col = jnp.sum(jnp.where(same & (at_col < at_row), 1, 0), axis=1, keepdims=True)
    return slot_row, cid_col, slot_col


def kernel(
    side,
    heads,
    grad_hbm,
    input_hbm,
    w_hbm,
    q_hbm,
    k_hbm,
    v_hbm,
    cid_hbm,
    grads_out,
    wg_out,
    grad_ref,
    input_ref,
    w_ref,
    qkv_ref,
    cid_ref,
    in_sem,
    ready,
    grad_land,
    pick,
    unpick,
    packed,
    split_ref,
    join_ref,
    send1,
    land2,
    back1,
    home,
    piece,
    turned0,
    turned1,
    both_ref,
    part_send0,
    part_send1,
    part_land0,
    part_land1,
    part_sum0,
    part_sum1,
    last_send0,
    last_send1,
    last_land0,
    last_land1,
    c_send,
    c_recv,
    x_send,
    x_recv,
    i_send,
    i_recv,
    s_send,
    s_recv,
    b_send,
    b_recv,
    h_send,
    h_recv,
    p_send,
    p_recv,
    l_send,
    l_recv,
):
    n = side
    tokens, cols = grad_ref.shape
    head_dim = w_ref.shape[0]
    clusters = n * n
    rows = clusters * MESSAGE
    scale = 1.0 / math.sqrt(head_dim)
    seq = lax.axis_index("seq")
    mp = lax.axis_index("mp")
    core = lax.rem(seq, 2)
    chip = seq // 2
    y = chip // n
    z = lax.rem(chip, n)
    other = seq + 1 - 2 * core
    row = lax.rem(y, 2)
    mine = row * 2 + core

    def in_pair(rows_on, cores_on):
        there = y + rows_on * (1 - 2 * row)
        return (there * n + z) * 2 + core + cores_on * (1 - 2 * core)

    pair = [(0, 1), (1, 0), (1, 1)]

    ys = [lax.rem(y + d, n) for d in range(n)]
    zs = [lax.rem(z + d, n) for d in range(n)]
    pair_rows = [y // 2 for y in ys]
    away = sorted(
        ((dy, dz) for dy in range(n) for dz in range(n) if dy or dz),
        key=lambda d: -min(d[0], n - d[0]) - min(d[1], n - d[1]),
    )

    sent = []

    barrier = pltpu.get_barrier_semaphore()

    def greet(to):
        pl.semaphore_signal(barrier, inc=1, device_id=to, device_id_type=MESH)

    for off in range(1, heads):
        greet((seq, lax.rem(mp + off, heads)))
        for on in pair:
            greet((in_pair(*on), lax.rem(mp + off, heads)))
    greet((other, mp))
    greet((in_pair(1, 1), mp))
    for d in range(1, n):
        greet(((ys[d] * n + z) * 2 + core, mp))
        greet(((y * n + zs[d]) * 2 + core, mp))
        greet(((y * n + zs[d]) * 2 + 1 - core, mp))
    fetches = [
        pltpu.make_async_copy(src, dst, in_sem.at[i])
        for i, (src, dst) in enumerate(
            (
                (grad_hbm, grad_ref),
                (w_hbm, w_ref),
                (cid_hbm, cid_ref.at[mine]),
                (q_hbm, qkv_ref.at[pl.ds(0, 1)]),
                (k_hbm, qkv_ref.at[pl.ds(1, 1)]),
                (v_hbm, qkv_ref.at[pl.ds(2, 1)]),
                (input_hbm, input_ref),
            )
        )
    ]
    for fetch in fetches:
        fetch.start()
    pl.semaphore_wait(barrier, 3 * (n - 1) + 2 + 4 * (heads - 1))

    def grad_copy(off):
        return copy_to(
            grad_ref,
            grad_land.at[off - 1],
            x_send.at[off - 1],
            x_recv.at[off - 1],
            (seq, lax.rem(mp + off, heads)),
        )

    fetches[0].wait()
    for off in range(1, heads):
        grad_copy(off).start()
        sent.append(grad_copy(off).wait_send)
    for d in range(1, n):
        pl.semaphore_signal(
            ready, inc=1, device_id=((ys[d] * n + z) * 2 + core, mp), device_id_type=MESH
        )
    fetches[2].wait()

    def cid_copy(i, of):
        return copy_to(
            cid_ref.at[of], cid_ref.at[of], c_send.at[i], c_recv.at[i], (in_pair(*pair[i]), mp)
        )

    for i in range(3):
        cid_copy(i, mine).start()
        sent.append(cid_copy(i, mine).wait_send)

    cid_row = cid_ref[mine]
    slot_row = slots(cid_row)[0]
    target_row = cid_row * MOST + slot_row
    r_col = iota((rows, 1), 0)
    key_col = (r_col // MESSAGE) * MOST + r_col % MOST
    kind_col = r_col // MOST % KINDS
    for i in range(3, 6):
        fetches[i].wait()
    total = None
    for kind in range(3):
        chosen = as_bf16(jnp.where(kind_col == kind, key_col, -1) == target_row)
        term = dot(chosen, qkv_ref[kind])
        total = term if total is None else total + term
    packed[...] = total
    pick[...] = as_bf16(jnp.where(kind_col == 3, key_col, -1) == target_row)

    def w_part(owner):
        return w_ref[:, pl.ds(pl.multiple_of(owner * cols, cols), cols)]

    fetches[1].wait()
    head_grad = dot(grad_ref[...], w_part(mp), NT)
    for off in sorted(range(1, heads), key=lambda d: min(d, heads - d)):
        grad_copy(off).wait_recv()
        head_grad += dot(grad_land[off - 1], w_part(lax.rem(mp + heads - off, heads)), NT)
    filled = packed[...] + dot(pick[...], head_grad.astype(BF16))
    send1[...] = filled.reshape(clusters, MESSAGE, head_dim).astype(BF16)
    pl.semaphore_wait(ready, n - 1)

    def to_owner(to):
        copy_to(
            send1.at[to], land2.at[seq], s_send.at[0], s_recv.at[0], (to * 2, mp)
        ).start()

    for dy, dz in away:
        to_owner(ys[dy] * n + zs[dz])

    @pl.when(core == 0)
    def _():
        land2[seq] = send1[chip]

    @pl.when(core == 1)
    def _():
        to_owner(chip)

    def owner_sent():
        @pl.when(core == 0)
        def _():
            take(send1.at[pl.ds(0, clusters - 1)], s_send.at[0])

        @pl.when(core == 1)
        def _():
            take(send1, s_send.at[0])

    sent.append(owner_sent)

    fetches[6].wait()
    wide = 2 * FEATS * n
    half = wide // 2
    out_row = iota((wide, wide), 0)
    in_row = iota((wide, wide), 1)
    out_at = out_row % half
    wanted = (out_at // FEATS) * 2 * FEATS + (out_row // half) * FEATS + out_at % FEATS
    order = as_bf16(wanted == in_row)
    blocks = cols // wide
    for i in range(blocks):
        done = dot(order, input_ref[:, i * wide : (i + 1) * wide], NT).astype(BF16)
        piece[i] = done.reshape(2, n, FEATS, tokens)

    for i, (rows_on, cores_on) in enumerate(pair):
        cid_copy(
            i, (row + rows_on * (1 - 2 * row)) * 2 + core + cores_on * (1 - 2 * core)
        ).wait_recv()
    home_rows = clusters // 2 * MESSAGE
    r_row = iota((1, home_rows), 1)
    key_row = r_row // MESSAGE * 2 * MOST + r_row % MOST
    kind_row = r_row // MOST % KINDS
    for of in range(4):
        _, cid_col, slot_col = slots(cid_ref[of])
        wanted = cid_col * MOST + slot_col
        for kind in range(3):
            for which in range(2):
                unpick[which, of, kind * tokens : (kind + 1) * tokens] = as_bf16(
                    jnp.where(kind_row == kind, key_row + MOST * which, -1) == wanted
                )

    def input_copy(off, to, received_of=None):
        at = (
            lax.rem(mp + heads - off, heads) if received_of is not None else mp
        )
        of = mine if received_of is None else received_of
        dst = turned0.at[of, at] if to % 2 == 0 else turned1.at[of, :, at]
        return copy_to(
            piece.at[to // 2, to % 2],
            dst,
            i_send.at[4 * off + to],
            i_recv.at[4 * off + of],
            ((((y // 2) * 2 + to // 2) * n + z) * 2 + to % 2, lax.rem(mp + off, heads)),
        )

    def inputs(act):
        for off in range(heads):
            for to in range(4):
                if off == 0:

                    @pl.when(mine != to)
                    def _():
                        act(off, to)
                else:
                    act(off, to)

    inputs(lambda off, to: input_copy(off, to).start())
    sent.append(lambda: inputs(lambda off, to: input_copy(off, to).wait_send()))

    @pl.when(core == 0)
    def _():
        turned0[mine, mp] = piece[row, 0]

    @pl.when(core == 1)
    def _():
        turned1[mine, :, mp] = piece[row, 1]

    count = 2 * clusters * MOST
    lot = min(256, 2 * rows)
    part = lot // KINDS
    lots = 2 * rows // lot
    out_row = iota((lot, lot), 0)
    in_row = iota((lot, lot), 1)
    out_at = out_row % part
    wanted = (out_at // 2) * MESSAGE + (out_row // part) * 2 + out_at % 2
    split_ref[...] = as_bf16(wanted == in_row)
    out_row = iota((lot, 3 * part), 0)
    in_row = iota((lot, 3 * part), 1)
    wanted = (out_row // 2 % 4) * part + (out_row // MESSAGE) * 2 + out_row % 2
    join_ref[...] = as_bf16(wanted == in_row)

    @pl.when(core == 0)
    def _():
        take(land2.at[pl.ds(0, 2 * clusters - 1)], s_recv.at[0])


    odd = lax.rem(chip, 2)
    even = odd == 0

    lot_home = clusters // 2
    spot = odd * lot_home + chip // 2

    def to_home(to_pair, to_y, to_z):
        copy_to(
            back1.at[to_pair, to_z],
            home.at[spot],
            b_send.at[0],
            b_recv.at[0],
            ((to_y * n + to_z) * 2 + odd, mp),
        ).start()

    @pl.when(core == 0)
    def _():
        got = land2[...].astype(F32).reshape(2 * rows, head_dim).astype(BF16)
        pieces = [[] for _ in range(KINDS)]
        for i in range(lots):
            parted = dot(split_ref[...], got[i * lot : (i + 1) * lot]).astype(BF16)
            for kind in range(KINDS):
                pieces[kind].append(parted[kind * part : (kind + 1) * part])
        queries, keys, values, grads = (jnp.concatenate(p, axis=0) for p in pieces)
        allowed = iota((count, count), 0) <= iota((count, count), 1)
        scores = jnp.where(allowed, dot(keys, queries, NT) * scale, -1e30)
        weights = jnp.exp(scores - jnp.max(scores, axis=0, keepdims=True))
        probs = weights / jnp.sum(weights, axis=0, keepdims=True)
        probs_low = probs.astype(BF16)
        prob_grad = dot(values, grads, NT)
        delta = jnp.sum(probs_low.astype(F32) * prob_grad, axis=0, keepdims=True)
        dscore = (probs * (prob_grad - delta)).astype(BF16)
        value_part = dot(probs_low, grads).astype(BF16)
        key_part = (dot(dscore, queries) * scale).astype(BF16)
        query_part = (dot(dscore, keys, TN) * scale).astype(BF16)
        outs = []
        for i in range(lots):
            span = slice(i * part, (i + 1) * part)
            three = jnp.concatenate([query_part[span], key_part[span], value_part[span]], axis=0)
            outs.append(dot(join_ref[...], three))
        whole = jnp.concatenate(outs, axis=0)
        whole = whole.reshape(n // 2, 2, n, 2, MESSAGE, head_dim).astype(BF16)
        for i in range(2):
            back1[:, :, i] = whole[:, i]

        for dy, dz in away:
            to_home(pair_rows[dy], ys[dy], zs[dz])

        @pl.when(even)
        def _():
            home[spot] = back1[y // 2, z]

        @pl.when(jnp.logical_not(even))
        def _():
            to_home(y // 2, y, z)

    def back_sent():
        @pl.when((core == 0) & even)
        def _():
            take(home.at[pl.ds(0, clusters - 1)], b_send.at[0])

        @pl.when((core == 0) & jnp.logical_not(even))
        def _():
            take(home, b_send.at[0])

    sent.append(back_sent)

    @pl.when((core == 0) & even)
    def _():
        take(home.at[pl.ds(0, lot_home - 1)], b_recv.at[0])

    @pl.when((core == 1) | jnp.logical_not(even))
    def _():
        take(home.at[pl.ds(0, lot_home)], b_recv.at[0])

    own_half = pl.ds(core * lot_home, lot_home)
    other_half = pl.ds((1 - core) * lot_home, lot_home)
    swap = copy_to(home.at[own_half], home.at[own_half], h_send.at[0], h_recv.at[0], (other, mp))
    swap.start()
    sent.append(swap.wait_send)

    def order_half(which, span, of):
        got = home[span, of // 2, of % 2].astype(F32).reshape(home_rows, head_dim).astype(BF16)
        return dot(unpick[which, of], got)

    first_half = [order_half(core, own_half, of) for of in range(4)]
    take(home.at[pl.ds(0, lot_home)], h_recv.at[0])

    for of in range(4):
        ordered = (first_half[of] + order_half(1 - core, other_half, of)).astype(BF16)
        for kind in range(3):
            both_ref[
                of * tokens : (of + 1) * tokens, kind * head_dim : (kind + 1) * head_dim
            ] = ordered[kind * tokens : (kind + 1) * tokens]
    for which in range(2):

        @pl.when(core == which)
        def _():
            for off in range(heads):
                for of in range(4):
                    if off or of % 2 != which:
                        input_copy(off, which, of).wait_recv()
                    else:

                        @pl.when(row != of // 2)
                        def _():
                            input_copy(off, which, of).wait_recv()

    class Sums:
        def __init__(self, which):
            in_y = (n // 2, pair_rows, lambda i: ((i * 2 + row) * n + z) * 2 + which)
            in_z = (n, zs, lambda i: (y * n + i) * 2 + which)
            self.first, self.second = (in_y, in_z) if which == 0 else (in_z, in_y)
            self.turned = (turned0, turned1)[which]
            self.part_send = (part_send0, part_send1)[which]
            self.part_land = (part_land0, part_land1)[which]
            self.part_sum = (part_sum0, part_sum1)[which]
            self.last_send = (last_send0, last_send1)[which]
            self.last_land = (last_land0, last_land1)[which]

        @staticmethod
        def places(axis):
            size, near, _ = axis
            steps = [rem_at(near, size, d) for d in range(size)]
            far = sorted(range(1, size), key=lambda d: -min(d, size - d))
            return [(d, steps[d], steps[size - d]) for d in far], steps[0]

        def part_copy(self, d, to, source):
            return copy_to(
                self.part_send.at[to],
                self.part_land.at[source],
                p_send.at[d],
                p_recv.at[d],
                (self.first[2](to), mp),
            )

        def last_copy(self, d, to, source):
            return copy_to(
                self.last_send.at[to],
                self.last_land.at[source],
                l_send.at[d],
                l_recv.at[d],
                (self.second[2](to), mp),
            )

        def partial(self, to, both):
            high = self.part_send.shape[1]
            left = [self.turned[of, to].reshape(high, tokens) for of in range(4)]
            return dot(jnp.concatenate(left, axis=1), both)

        def begin(self):
            both = both_ref[...]
            others, here = self.places(self.first)
            for d, to, _ in others:
                self.part_send[to] = self.partial(to, both).astype(BF16)
                self.part_copy(d, to, here).start()
            self.part_sum[...] = self.partial(here, both).reshape(self.part_sum.shape)

        def finish(self):
            others, here = self.places(self.first)
            for d, _, source in reversed(others):
                self.part_copy(d, here, source).wait_recv()
                self.part_sum[...] += (
                    self.part_land[source].astype(F32).reshape(self.part_sum.shape)
                )
            self.last_send[...] = self.part_sum[...].astype(BF16)
            lasts, last_here = self.places(self.second)
            for d, to, _ in lasts:
                self.last_copy(d, to, last_here).start()
            wg_out[...] = self.part_sum[last_here]
            for d, to, _ in others:
                self.part_copy(d, to, here).wait_send()
            for d, _, source in reversed(lasts):
                self.last_copy(d, last_here, source).wait_recv()
                wg_out[...] += self.last_land[source].astype(F32)
            for d, to, _ in lasts:
                self.last_copy(d, to, last_here).wait_send()

    def rem_at(near, size, d):
        return near[d] if size == n else near[2 * d]

    for which in range(2):

        @pl.when(core == which)
        def _():
            Sums(which).begin()

    for kind in range(3):
        span = slice(kind * head_dim, (kind + 1) * head_dim)
        grads_out[kind] = both_ref[pl.ds(pl.multiple_of(mine * tokens, tokens), tokens), span]
    for wait_sent in sent:
        wait_sent()

    for which in range(2):

        @pl.when(core == which)
        def _():
            Sums(which).finish()


def hand_out(grads_in, wg_in, dq_out, dk_out, dv_out, wg_out, sem):
    copies = [
        pltpu.make_async_copy(grads_in.at[pl.ds(kind, 1)], out, sem.at[kind])
        for kind, out in enumerate((dq_out, dk_out, dv_out))
    ]
    copies.append(pltpu.make_async_copy(wg_in, wg_out, sem.at[3]))
    for copy in copies:
        copy.start()
    for copy in copies:
        copy.wait()


def on_device(layer_input, output_grad, w_out, query_heads, key_heads, value_heads, cluster_ids):
    devices = lax.axis_size("seq")
    heads = lax.axis_size("mp")
    n = math.isqrt(devices // 2)
    tokens, cols = layer_input.shape
    head_dim = query_heads.shape[2]
    clusters = n * n
    rows = clusters * MESSAGE
    half = FEATS * n
    lot = min(256, 2 * rows)
    width = 3 * head_dim
    vmem = pl.BlockSpec(memory_space=pltpu.VMEM)
    hbm = pl.BlockSpec(memory_space=pltpu.HBM)
    dma = pltpu.SemaphoreType.DMA
    grad_shape = jax.ShapeDtypeStruct((1, tokens, head_dim), BF16)
    wg_shape = jax.ShapeDtypeStruct((FEATS, width), F32)
    grads, weight_grad = pl.pallas_call(
        lambda *refs: kernel(n, heads, *refs),
        out_shape=(
            pltpu.VMEM((3, tokens, head_dim), BF16),
            pltpu.VMEM((FEATS, width), F32),
        ),
        in_specs=[hbm] * 7,
        out_specs=(vmem, vmem),
        scratch_shapes=[
            pltpu.VMEM((tokens, cols), BF16),
            pltpu.VMEM((tokens, cols), BF16),
            pltpu.VMEM((head_dim, heads * cols), BF16),
            pltpu.VMEM((3, tokens, head_dim), BF16),
            pltpu.VMEM((4, 1, tokens), jnp.int32),
            dma((7,)),
            pltpu.SemaphoreType.REGULAR,
            pltpu.VMEM((heads - 1, tokens, cols), BF16),
            pltpu.VMEM((rows, tokens), BF16),
            pltpu.VMEM((2, 4, 3 * tokens, rows // 2), BF16),
            pltpu.VMEM((rows, head_dim), F32),
            pltpu.VMEM((lot, lot), BF16),
            pltpu.VMEM((lot, 3 * lot // KINDS), BF16),
            pltpu.VMEM((clusters, MESSAGE, head_dim), BF16),
            pltpu.VMEM((2 * clusters, MESSAGE, head_dim), BF16),
            pltpu.VMEM((n // 2, n, 2, 2, MESSAGE, head_dim), BF16),
            pltpu.VMEM((clusters, 2, 2, MESSAGE, head_dim), BF16),
            pltpu.VMEM((2, 2, n, FEATS, tokens), BF16),
            pltpu.VMEM((4, n // 2, n, FEATS, tokens), BF16),
            pltpu.VMEM((4, n, n // 2, FEATS, tokens), BF16),
            pltpu.VMEM((4 * tokens, width), BF16),
            pltpu.VMEM((n // 2, half, width), BF16),
            pltpu.VMEM((n, half // 2, width), BF16),
            pltpu.VMEM((n // 2, half, width), BF16),
            pltpu.VMEM((n, half // 2, width), BF16),
            pltpu.VMEM((n, FEATS, width), F32),
            pltpu.VMEM((n // 2, FEATS, width), F32),
            pltpu.VMEM((n, FEATS, width), BF16),
            pltpu.VMEM((n // 2, FEATS, width), BF16),
            pltpu.VMEM((n, FEATS, width), BF16),
            pltpu.VMEM((n // 2, FEATS, width), BF16),
            dma((3,)),
            dma((3,)),
            dma((heads - 1,)),
            dma((heads - 1,)),
            dma((4 * heads,)),
            dma((4 * heads,)),
            dma((1,)),
            dma((1,)),
            dma((1,)),
            dma((1,)),
            dma((1,)),
            dma((1,)),
            dma((n,)),
            dma((n,)),
            dma((n,)),
            dma((n,)),
        ],
        compiler_params=pltpu.CompilerParams(
            collective_id=0, has_side_effects=True, vmem_limit_bytes=40 * 1024 * 1024
        ),
    )(
        *(
            pltpu.with_memory_space_constraint(x, pltpu.HBM)
            for x in (
                output_grad,
                layer_input,
                w_out,
                query_heads,
                key_heads,
                value_heads,
                cluster_ids.reshape(1, tokens),
            )
        )
    )
    return pl.pallas_call(
        hand_out,
        out_shape=(grad_shape, grad_shape, grad_shape, wg_shape),
        in_specs=[vmem] * 2,
        out_specs=(hbm,) * 4,
        scratch_shapes=[dma((4,))],
        compiler_params=pltpu.CompilerParams(vmem_limit_bytes=16 * 1024 * 1024),
    )(grads, weight_grad)


def solution(mesh):
    return jax.shard_map(
        on_device,
        mesh=mesh,
        in_specs=(
            P("seq", "mp"),
            P("seq", "mp"),
            P("mp", None),
            P("mp", "seq", None),
            P("mp", "seq", None),
            P("mp", "seq", None),
            P("mp", "seq", None),
        ),
        out_specs=(
            P("mp", "seq", None),
            P("mp", "seq", None),
            P("mp", "seq", None),
            P("seq", "mp"),
        ),
        check_vma=False,
    )
```

```python
import math

import jax
import jax.numpy as jnp
from jax import lax
from jax.experimental import pallas as pl
from jax.experimental.pallas import tpu as pltpu
from jax.sharding import PartitionSpec as P

MOST = 2
KINDS = 4
MESSAGE = MOST * KINDS
FEATS = 16
MESH = pl.DeviceIdType.MESH
F32 = jnp.float32
BF16 = jnp.bfloat16
NT = (((1,), (1,)), ((), ()))
TN = (((0,), (0,)), ((), ()))


def dot(left, right, dims=(((1,), (0,)), ((), ()))):
    return lax.dot_general(left, right, dims, preferred_element_type=F32)


def iota(shape, dim):
    return lax.broadcasted_iota(jnp.int32, shape, dim)


def as_bf16(mask):
    return jnp.where(mask, 1.0, 0.0).astype(BF16)


def copy_to(src, dst, send_sem, recv_sem, device):
    return pltpu.make_async_remote_copy(
        src_ref=src,
        dst_ref=dst,
        send_sem=send_sem,
        recv_sem=recv_sem,
        device_id=device,
        device_id_type=MESH,
    )


def take(ref, sem):
    pltpu.make_async_copy(ref, ref, sem).wait()


def slots(cid_row):
    tokens = cid_row.shape[1]
    across = jnp.broadcast_to(cid_row, (tokens, tokens))
    at_row = iota((tokens, tokens), 0)
    at_col = iota((tokens, tokens), 1)
    cid_col = jnp.sum(jnp.where(at_row == at_col, across, 0), axis=1, keepdims=True)
    same = across == cid_col
    slot_row = jnp.sum(jnp.where(same & (at_row < at_col), 1, 0), axis=0, keepdims=True)
    slot_col = jnp.sum(jnp.where(same & (at_col < at_row), 1, 0), axis=1, keepdims=True)
    return slot_row, cid_col, slot_col


def kernel(
    side,
    heads,
    grad_hbm,
    input_hbm,
    w_hbm,
    q_hbm,
    k_hbm,
    v_hbm,
    cid_hbm,
    grads_out,
    wg_out,
    grad_ref,
    input_ref,
    w_ref,
    qkv_ref,
    cid_ref,
    in_sem,
    ready,
    grad_land,
    pick,
    unpick,
    packed,
    split_ref,
    mask_ref,
    send1,
    land2,
    back1,
    home,
    piece,
    turned0,
    turned1,
    both_ref,
    part_send0,
    part_send1,
    part_land0,
    part_land1,
    part_sum0,
    part_sum1,
    last_send0,
    last_send1,
    last_land0,
    last_land1,
    c_send,
    c_recv,
    x_send,
    x_recv,
    i_send,
    i_recv,
    s_send,
    s_recv,
    b_send,
    b_recv,
    h_send,
    h_recv,
    p_send,
    p_recv,
    l_send,
    l_recv,
):
    n = side
    tokens, cols = grad_ref.shape
    head_dim = w_ref.shape[0]
    clusters = n * n
    rows = clusters * MESSAGE
    scale = 1.0 / math.sqrt(head_dim)
    seq = lax.axis_index("seq")
    mp = lax.axis_index("mp")
    core = lax.rem(seq, 2)
    chip = seq // 2
    y = chip // n
    z = lax.rem(chip, n)
    other = seq + 1 - 2 * core
    row = lax.rem(y, 2)
    mine = row * 2 + core

    def in_pair(rows_on, cores_on):
        there = y + rows_on * (1 - 2 * row)
        return (there * n + z) * 2 + core + cores_on * (1 - 2 * core)

    pair = [(0, 1), (1, 0), (1, 1)]

    ys = [lax.rem(y + d, n) for d in range(n)]
    zs = [lax.rem(z + d, n) for d in range(n)]
    pair_rows = [y // 2 for y in ys]
    away = sorted(
        ((dy, dz) for dy in range(n) for dz in range(n) if dy or dz),
        key=lambda d: -min(d[0], n - d[0]) - min(d[1], n - d[1]),
    )

    sent = []

    barrier = pltpu.get_barrier_semaphore()

    def greet(to):
        pl.semaphore_signal(barrier, inc=1, device_id=to, device_id_type=MESH)

    for off in range(1, heads):
        greet((seq, lax.rem(mp + off, heads)))
        for on in pair:
            greet((in_pair(*on), lax.rem(mp + off, heads)))
    greet((other, mp))
    greet((in_pair(1, 1), mp))
    for d in range(1, n):
        greet(((ys[d] * n + z) * 2 + core, mp))
        greet(((y * n + zs[d]) * 2 + core, mp))
        greet(((y * n + zs[d]) * 2 + 1 - core, mp))
    fetches = [
        pltpu.make_async_copy(src, dst, in_sem.at[i])
        for i, (src, dst) in enumerate(
            (
                (grad_hbm, grad_ref),
                (w_hbm, w_ref),
                (cid_hbm, cid_ref.at[mine]),
                (q_hbm, qkv_ref.at[pl.ds(0, 1)]),
                (k_hbm, qkv_ref.at[pl.ds(1, 1)]),
                (v_hbm, qkv_ref.at[pl.ds(2, 1)]),
                (input_hbm, input_ref),
            )
        )
    ]
    for fetch in fetches:
        fetch.start()
    pl.semaphore_wait(barrier, 3 * (n - 1) + 2 + 4 * (heads - 1))

    def grad_copy(off):
        return copy_to(
            grad_ref,
            grad_land.at[off - 1],
            x_send.at[off - 1],
            x_recv.at[off - 1],
            (seq, lax.rem(mp + off, heads)),
        )

    fetches[0].wait()
    for off in range(1, heads):
        grad_copy(off).start()
        sent.append(grad_copy(off).wait_send)
    for d in range(1, n):
        pl.semaphore_signal(
            ready, inc=1, device_id=((ys[d] * n + z) * 2 + core, mp), device_id_type=MESH
        )
    fetches[2].wait()

    def cid_copy(i, of):
        return copy_to(
            cid_ref.at[of], cid_ref.at[of], c_send.at[i], c_recv.at[i], (in_pair(*pair[i]), mp)
        )

    for i in range(3):
        cid_copy(i, mine).start()
        sent.append(cid_copy(i, mine).wait_send)

    cid_row = cid_ref[mine]
    slot_row = slots(cid_row)[0]
    target_row = cid_row * MOST + slot_row
    r_col = iota((rows, 1), 0)
    key_col = (r_col // MESSAGE) * MOST + r_col % MOST
    kind_col = r_col // MOST % KINDS
    for i in range(3, 6):
        fetches[i].wait()
    total = None
    for kind in range(3):
        chosen = as_bf16(jnp.where(kind_col == kind, key_col, -1) == target_row)
        term = dot(chosen, qkv_ref[kind])
        total = term if total is None else total + term
    packed[...] = total
    pick[...] = as_bf16(jnp.where(kind_col == 3, key_col, -1) == target_row)

    def w_part(owner):
        return w_ref[:, pl.ds(pl.multiple_of(owner * cols, cols), cols)]

    fetches[1].wait()
    head_grad = dot(grad_ref[...], w_part(mp), NT)
    for off in sorted(range(1, heads), key=lambda d: min(d, heads - d)):
        grad_copy(off).wait_recv()
        head_grad += dot(grad_land[off - 1], w_part(lax.rem(mp + heads - off, heads)), NT)
    filled = packed[...] + dot(pick[...], head_grad.astype(BF16))
    send1[...] = filled.reshape(clusters, MESSAGE, head_dim).astype(BF16)
    pl.semaphore_wait(ready, n - 1)

    def to_owner(to):
        copy_to(
            send1.at[to], land2.at[seq], s_send.at[0], s_recv.at[0], (to * 2, mp)
        ).start()

    for dy, dz in away:
        to_owner(ys[dy] * n + zs[dz])

    @pl.when(core == 0)
    def _():
        land2[seq] = send1[chip]

    @pl.when(core == 1)
    def _():
        to_owner(chip)

    def owner_sent():
        @pl.when(core == 0)
        def _():
            take(send1.at[pl.ds(0, clusters - 1)], s_send.at[0])

        @pl.when(core == 1)
        def _():
            take(send1, s_send.at[0])

    sent.append(owner_sent)

    fetches[6].wait()
    wide = 2 * FEATS * n
    half = wide // 2
    out_row = iota((wide, wide), 0)
    in_row = iota((wide, wide), 1)
    out_at = out_row % half
    wanted = (out_at // FEATS) * 2 * FEATS + (out_row // half) * FEATS + out_at % FEATS
    order = as_bf16(wanted == in_row)
    blocks = cols // wide
    for i in range(blocks):
        done = dot(order, input_ref[:, i * wide : (i + 1) * wide], NT).astype(BF16)
        piece[i] = done.reshape(2, n, FEATS, tokens)

    for i, (rows_on, cores_on) in enumerate(pair):
        cid_copy(
            i, (row + rows_on * (1 - 2 * row)) * 2 + core + cores_on * (1 - 2 * core)
        ).wait_recv()
    home_rows = clusters // 2 * 4 * MOST
    r_row = iota((1, home_rows), 1)
    key_row = r_row // (4 * MOST) * 8 * MOST + r_row % (4 * MOST)
    for of in range(4):
        _, cid_col, slot_col = slots(cid_ref[of])
        wanted = (cid_col * 4 + of) * MOST + slot_col
        for which in range(2):
            unpick[which, of * tokens : (of + 1) * tokens] = as_bf16(
                key_row + 4 * MOST * which == wanted
            )

    def input_copy(off, to, received_of=None):
        at = (
            lax.rem(mp + heads - off, heads) if received_of is not None else mp
        )
        of = mine if received_of is None else received_of
        dst = turned0.at[of, at] if to % 2 == 0 else turned1.at[of, :, at]
        return copy_to(
            piece.at[to // 2, to % 2],
            dst,
            i_send.at[4 * off + to],
            i_recv.at[4 * off + of],
            ((((y // 2) * 2 + to // 2) * n + z) * 2 + to % 2, lax.rem(mp + off, heads)),
        )

    def inputs(act):
        for off in range(heads):
            for to in range(4):
                if off == 0:

                    @pl.when(mine != to)
                    def _():
                        act(off, to)
                else:
                    act(off, to)

    inputs(lambda off, to: input_copy(off, to).start())
    sent.append(lambda: inputs(lambda off, to: input_copy(off, to).wait_send()))

    @pl.when(core == 0)
    def _():
        turned0[mine, mp] = piece[row, 0]

    @pl.when(core == 1)
    def _():
        turned1[mine, :, mp] = piece[row, 1]

    count = 2 * clusters * MOST
    lot = min(256, 2 * rows)
    part = lot // KINDS
    lots = 2 * rows // lot
    out_row = iota((lot, lot), 0)
    in_row = iota((lot, lot), 1)

    def source(p):
        first = p // (4 * MOST * n)
        second = p // (4 * MOST) % n
        return ((first * 2 + p // (2 * MOST) % 2) * n + second) * 2 * MOST + p % (2 * MOST)

    token = source(out_row % part)
    wanted = (token // MOST) * MESSAGE + (out_row // part) * MOST + token % MOST
    split_ref[...] = as_bf16(wanted == in_row)
    mask_ref[...] = jnp.where(
        source(iota((count, 1), 0)) <= source(iota((1, count), 1)), 0.0, -1e30
    )

    @pl.when(core == 0)
    def _():
        take(land2.at[pl.ds(0, 2 * clusters - 1)], s_recv.at[0])


    odd = lax.rem(chip, 2)
    even = odd == 0

    lot_home = clusters // 2
    spot = odd * lot_home + chip // 2

    def to_home(to_pair, to_y, to_z):
        copy_to(
            back1.at[to_pair * n + to_z],
            home.at[spot],
            b_send.at[0],
            b_recv.at[0],
            ((to_y * n + to_z) * 2 + odd, mp),
        ).start()

    @pl.when(core == 0)
    def _():
        got = land2[...].astype(F32).reshape(2 * rows, head_dim).astype(BF16)
        pieces = [[] for _ in range(KINDS)]
        for i in range(lots):
            parted = dot(split_ref[...], got[i * lot : (i + 1) * lot]).astype(BF16)
            for kind in range(KINDS):
                pieces[kind].append(parted[kind * part : (kind + 1) * part])
        queries, keys, values, grads = (jnp.concatenate(p, axis=0) for p in pieces)
        scores = jnp.where(mask_ref[...] < 0, -1e30, dot(keys, queries, NT) * scale)
        weights = jnp.exp(scores - jnp.max(scores, axis=0, keepdims=True))
        probs = weights / jnp.sum(weights, axis=0, keepdims=True)
        probs_low = probs.astype(BF16)
        prob_grad = dot(values, grads, NT)
        delta = jnp.sum(probs_low.astype(F32) * prob_grad, axis=0, keepdims=True)
        dscore = (probs * (prob_grad - delta)).astype(BF16)
        parts = (
            dot(dscore, keys, TN) * scale,
            dot(dscore, queries) * scale,
            dot(probs_low, grads),
        )
        for kind in range(3):
            back1[:, kind] = parts[kind].reshape(-1, 4 * MOST, head_dim).astype(BF16)

        for dy, dz in away:
            to_home(pair_rows[dy], ys[dy], zs[dz])

        @pl.when(even)
        def _():
            home[spot] = back1[y // 2 * n + z]

        @pl.when(jnp.logical_not(even))
        def _():
            to_home(y // 2, y, z)

    def back_sent():
        @pl.when((core == 0) & even)
        def _():
            take(home.at[pl.ds(0, clusters - 1)], b_send.at[0])

        @pl.when((core == 0) & jnp.logical_not(even))
        def _():
            take(home, b_send.at[0])

    sent.append(back_sent)

    @pl.when((core == 0) & even)
    def _():
        take(home.at[pl.ds(0, lot_home - 1)], b_recv.at[0])

    @pl.when((core == 1) | jnp.logical_not(even))
    def _():
        take(home.at[pl.ds(0, lot_home)], b_recv.at[0])

    own_half = pl.ds(core * lot_home, lot_home)
    other_half = pl.ds((1 - core) * lot_home, lot_home)
    swap = copy_to(home.at[own_half], home.at[own_half], h_send.at[0], h_recv.at[0], (other, mp))
    swap.start()
    sent.append(swap.wait_send)

    def order_half(which, span, kind):
        got = home[span, kind].astype(F32).reshape(home_rows, head_dim).astype(BF16)
        return dot(unpick[which], got)

    first_half = [order_half(core, own_half, kind) for kind in range(3)]
    take(home.at[pl.ds(0, lot_home)], h_recv.at[0])

    for kind in range(3):
        ordered = first_half[kind] + order_half(1 - core, other_half, kind)
        both_ref[:, kind * head_dim : (kind + 1) * head_dim] = ordered.astype(BF16)
    for which in range(2):

        @pl.when(core == which)
        def _():
            for off in range(heads):
                for of in range(4):
                    if off or of % 2 != which:
                        input_copy(off, which, of).wait_recv()
                    else:

                        @pl.when(row != of // 2)
                        def _():
                            input_copy(off, which, of).wait_recv()

    class Sums:
        def __init__(self, which):
            in_y = (n // 2, pair_rows, lambda i: ((i * 2 + row) * n + z) * 2 + which)
            in_z = (n, zs, lambda i: (y * n + i) * 2 + which)
            self.first, self.second = (in_y, in_z) if which == 0 else (in_z, in_y)
            self.turned = (turned0, turned1)[which]
            self.part_send = (part_send0, part_send1)[which]
            self.part_land = (part_land0, part_land1)[which]
            self.part_sum = (part_sum0, part_sum1)[which]
            self.last_send = (last_send0, last_send1)[which]
            self.last_land = (last_land0, last_land1)[which]

        @staticmethod
        def places(axis):
            size, near, _ = axis
            steps = [rem_at(near, size, d) for d in range(size)]
            far = sorted(range(1, size), key=lambda d: -min(d, size - d))
            return [(d, steps[d], steps[size - d]) for d in far], steps[0]

        def part_copy(self, d, to, source):
            return copy_to(
                self.part_send.at[to],
                self.part_land.at[source],
                p_send.at[d],
                p_recv.at[d],
                (self.first[2](to), mp),
            )

        def last_copy(self, d, to, source):
            return copy_to(
                self.last_send.at[to],
                self.last_land.at[source],
                l_send.at[d],
                l_recv.at[d],
                (self.second[2](to), mp),
            )

        def partial(self, to, both):
            high = self.part_send.shape[1]
            left = [self.turned[of, to].reshape(high, tokens) for of in range(4)]
            return dot(jnp.concatenate(left, axis=1), both)

        def begin(self):
            both = both_ref[...]
            others, here = self.places(self.first)
            for d, to, _ in others:
                self.part_send[to] = self.partial(to, both).astype(BF16)
                self.part_copy(d, to, here).start()
            self.part_sum[...] = self.partial(here, both).reshape(self.part_sum.shape)

        def finish(self):
            others, here = self.places(self.first)
            for d, _, source in reversed(others):
                self.part_copy(d, here, source).wait_recv()
                self.part_sum[...] += (
                    self.part_land[source].astype(F32).reshape(self.part_sum.shape)
                )
            self.last_send[...] = self.part_sum[...].astype(BF16)
            lasts, last_here = self.places(self.second)
            for d, to, _ in lasts:
                self.last_copy(d, to, last_here).start()
            wg_out[...] = self.part_sum[last_here]
            for d, to, _ in others:
                self.part_copy(d, to, here).wait_send()
            for d, _, source in reversed(lasts):
                self.last_copy(d, last_here, source).wait_recv()
                wg_out[...] += self.last_land[source].astype(F32)
            for d, to, _ in lasts:
                self.last_copy(d, to, last_here).wait_send()

    def rem_at(near, size, d):
        return near[d] if size == n else near[2 * d]

    for which in range(2):

        @pl.when(core == which)
        def _():
            Sums(which).begin()

    for kind in range(3):
        span = slice(kind * head_dim, (kind + 1) * head_dim)
        grads_out[kind] = both_ref[pl.ds(pl.multiple_of(mine * tokens, tokens), tokens), span]
    for wait_sent in sent:
        wait_sent()

    for which in range(2):

        @pl.when(core == which)
        def _():
            Sums(which).finish()


def hand_out(grads_in, wg_in, dq_out, dk_out, dv_out, wg_out, sem):
    copies = [
        pltpu.make_async_copy(grads_in.at[pl.ds(kind, 1)], out, sem.at[kind])
        for kind, out in enumerate((dq_out, dk_out, dv_out))
    ]
    copies.append(pltpu.make_async_copy(wg_in, wg_out, sem.at[3]))
    for copy in copies:
        copy.start()
    for copy in copies:
        copy.wait()


def on_device(layer_input, output_grad, w_out, query_heads, key_heads, value_heads, cluster_ids):
    devices = lax.axis_size("seq")
    heads = lax.axis_size("mp")
    n = math.isqrt(devices // 2)
    tokens, cols = layer_input.shape
    head_dim = query_heads.shape[2]
    clusters = n * n
    rows = clusters * MESSAGE
    half = FEATS * n
    lot = min(256, 2 * rows)
    width = 3 * head_dim
    vmem = pl.BlockSpec(memory_space=pltpu.VMEM)
    hbm = pl.BlockSpec(memory_space=pltpu.HBM)
    dma = pltpu.SemaphoreType.DMA
    grad_shape = jax.ShapeDtypeStruct((1, tokens, head_dim), BF16)
    wg_shape = jax.ShapeDtypeStruct((FEATS, width), F32)
    grads, weight_grad = pl.pallas_call(
        lambda *refs: kernel(n, heads, *refs),
        out_shape=(
            pltpu.VMEM((3, tokens, head_dim), BF16),
            pltpu.VMEM((FEATS, width), F32),
        ),
        in_specs=[hbm] * 7,
        out_specs=(vmem, vmem),
        scratch_shapes=[
            pltpu.VMEM((tokens, cols), BF16),
            pltpu.VMEM((tokens, cols), BF16),
            pltpu.VMEM((head_dim, heads * cols), BF16),
            pltpu.VMEM((3, tokens, head_dim), BF16),
            pltpu.VMEM((4, 1, tokens), jnp.int32),
            dma((7,)),
            pltpu.SemaphoreType.REGULAR,
            pltpu.VMEM((heads - 1, tokens, cols), BF16),
            pltpu.VMEM((rows, tokens), BF16),
            pltpu.VMEM((2, 4 * tokens, rows // 2), BF16),
            pltpu.VMEM((rows, head_dim), F32),
            pltpu.VMEM((lot, lot), BF16),
            pltpu.VMEM((2 * clusters * MOST, 2 * clusters * MOST), F32),
            pltpu.VMEM((clusters, MESSAGE, head_dim), BF16),
            pltpu.VMEM((2 * clusters, MESSAGE, head_dim), BF16),
            pltpu.VMEM((clusters // 2, 3, 4 * MOST, head_dim), BF16),
            pltpu.VMEM((clusters, 3, 4 * MOST, head_dim), BF16),
            pltpu.VMEM((2, 2, n, FEATS, tokens), BF16),
            pltpu.VMEM((4, n // 2, n, FEATS, tokens), BF16),
            pltpu.VMEM((4, n, n // 2, FEATS, tokens), BF16),
            pltpu.VMEM((4 * tokens, width), BF16),
            pltpu.VMEM((n // 2, half, width), BF16),
            pltpu.VMEM((n, half // 2, width), BF16),
            pltpu.VMEM((n // 2, half, width), BF16),
            pltpu.VMEM((n, half // 2, width), BF16),
            pltpu.VMEM((n, FEATS, width), F32),
            pltpu.VMEM((n // 2, FEATS, width), F32),
            pltpu.VMEM((n, FEATS, width), BF16),
            pltpu.VMEM((n // 2, FEATS, width), BF16),
            pltpu.VMEM((n, FEATS, width), BF16),
            pltpu.VMEM((n // 2, FEATS, width), BF16),
            dma((3,)),
            dma((3,)),
            dma((heads - 1,)),
            dma((heads - 1,)),
            dma((4 * heads,)),
            dma((4 * heads,)),
            dma((1,)),
            dma((1,)),
            dma((1,)),
            dma((1,)),
            dma((1,)),
            dma((1,)),
            dma((n,)),
            dma((n,)),
            dma((n,)),
            dma((n,)),
        ],
        compiler_params=pltpu.CompilerParams(
            collective_id=0, has_side_effects=True, vmem_limit_bytes=40 * 1024 * 1024
        ),
    )(
        *(
            pltpu.with_memory_space_constraint(x, pltpu.HBM)
            for x in (
                output_grad,
                layer_input,
                w_out,
                query_heads,
                key_heads,
                value_heads,
                cluster_ids.reshape(1, tokens),
            )
        )
    )
    return pl.pallas_call(
        hand_out,
        out_shape=(grad_shape, grad_shape, grad_shape, wg_shape),
        in_specs=[vmem] * 2,
        out_specs=(hbm,) * 4,
        scratch_shapes=[dma((4,))],
        compiler_params=pltpu.CompilerParams(vmem_limit_bytes=16 * 1024 * 1024),
    )(grads, weight_grad)


def solution(mesh):
    return jax.shard_map(
        on_device,
        mesh=mesh,
        in_specs=(
            P("seq", "mp"),
            P("seq", "mp"),
            P("mp", None),
            P("mp", "seq", None),
            P("mp", "seq", None),
            P("mp", "seq", None),
            P("mp", "seq", None),
        ),
        out_specs=(
            P("mp", "seq", None),
            P("mp", "seq", None),
            P("mp", "seq", None),
            P("seq", "mp"),
        ),
        check_vma=False,
    )
```

```python
import math

import jax
import jax.numpy as jnp
from jax import lax
from jax.experimental import pallas as pl
from jax.experimental.pallas import tpu as pltpu
from jax.sharding import PartitionSpec as P

MOST = 2
KINDS = 4
MESSAGE = MOST * KINDS
FEATS = 16
MESH = pl.DeviceIdType.MESH
F32 = jnp.float32
BF16 = jnp.bfloat16
NT = (((1,), (1,)), ((), ()))
TN = (((0,), (0,)), ((), ()))


def dot(left, right, dims=(((1,), (0,)), ((), ()))):
    return lax.dot_general(left, right, dims, preferred_element_type=F32)


def iota(shape, dim):
    return lax.broadcasted_iota(jnp.int32, shape, dim)


def as_bf16(mask):
    return jnp.where(mask, 1.0, 0.0).astype(BF16)


def copy_to(src, dst, send_sem, recv_sem, device):
    return pltpu.make_async_remote_copy(
        src_ref=src,
        dst_ref=dst,
        send_sem=send_sem,
        recv_sem=recv_sem,
        device_id=device,
        device_id_type=MESH,
    )


def take(ref, sem):
    pltpu.make_async_copy(ref, ref, sem).wait()


def slots(cid_row):
    tokens = cid_row.shape[1]
    across = jnp.broadcast_to(cid_row, (tokens, tokens))
    at_row = iota((tokens, tokens), 0)
    at_col = iota((tokens, tokens), 1)
    cid_col = jnp.sum(jnp.where(at_row == at_col, across, 0), axis=1, keepdims=True)
    same = across == cid_col
    slot_row = jnp.sum(jnp.where(same & (at_row < at_col), 1, 0), axis=0, keepdims=True)
    slot_col = jnp.sum(jnp.where(same & (at_col < at_row), 1, 0), axis=1, keepdims=True)
    return slot_row, cid_col, slot_col


def kernel(
    side,
    heads,
    grad_hbm,
    input_hbm,
    w_hbm,
    q_hbm,
    k_hbm,
    v_hbm,
    cid_hbm,
    grads_out,
    wg_out,
    grad_ref,
    input_ref,
    w_ref,
    qkv_ref,
    cid_ref,
    in_sem,
    ready,
    grad_land,
    pick,
    unpick,
    packed,
    split_ref,
    mask_ref,
    send1,
    land2,
    back1,
    home,
    piece,
    turned0,
    turned1,
    both_ref,
    part_send0,
    part_send1,
    part_land0,
    part_land1,
    part_sum0,
    part_sum1,
    last_send0,
    last_send1,
    last_land0,
    last_land1,
    c_send,
    c_recv,
    x_send,
    x_recv,
    i_send,
    i_recv,
    s_send,
    s_recv,
    b_send,
    b_recv,
    h_send,
    h_recv,
    p_send,
    p_recv,
    l_send,
    l_recv,
):
    n = side
    tokens, cols = grad_ref.shape
    head_dim = w_ref.shape[0]
    clusters = n * n
    rows = clusters * MESSAGE
    scale = 1.0 / math.sqrt(head_dim)
    seq = lax.axis_index("seq")
    mp = lax.axis_index("mp")
    core = lax.rem(seq, 2)
    chip = seq // 2
    y = chip // n
    z = lax.rem(chip, n)
    other = seq + 1 - 2 * core
    row = lax.rem(y, 2)
    mine = row * 2 + core

    def in_pair(rows_on, cores_on):
        there = y + rows_on * (1 - 2 * row)
        return (there * n + z) * 2 + core + cores_on * (1 - 2 * core)

    pair = [(0, 1), (1, 0), (1, 1)]

    ys = [lax.rem(y + d, n) for d in range(n)]
    zs = [lax.rem(z + d, n) for d in range(n)]
    pair_rows = [y // 2 for y in ys]
    away = sorted(
        ((dy, dz) for dy in range(n) for dz in range(n) if dy or dz),
        key=lambda d: -min(d[0], n - d[0]) - min(d[1], n - d[1]),
    )

    sent = []

    barrier = pltpu.get_barrier_semaphore()

    def greet(to):
        pl.semaphore_signal(barrier, inc=1, device_id=to, device_id_type=MESH)

    for off in range(1, heads):
        greet((seq, lax.rem(mp + off, heads)))
        for on in pair:
            greet((in_pair(*on), lax.rem(mp + off, heads)))
    greet((other, mp))
    greet((in_pair(1, 1), mp))
    for d in range(1, n):
        greet(((ys[d] * n + z) * 2 + core, mp))
        greet(((y * n + zs[d]) * 2 + core, mp))
        greet(((y * n + zs[d]) * 2 + 1 - core, mp))
    fetches = [
        pltpu.make_async_copy(src, dst, in_sem.at[i])
        for i, (src, dst) in enumerate(
            (
                (grad_hbm, grad_ref),
                (w_hbm, w_ref),
                (cid_hbm, cid_ref.at[mine]),
                (q_hbm, qkv_ref.at[pl.ds(0, 1)]),
                (k_hbm, qkv_ref.at[pl.ds(1, 1)]),
                (v_hbm, qkv_ref.at[pl.ds(2, 1)]),
                (input_hbm, input_ref),
            )
        )
    ]
    for fetch in fetches:
        fetch.start()
    pl.semaphore_wait(barrier, 3 * (n - 1) + 2 + 4 * (heads - 1))

    def grad_copy(off):
        return copy_to(
            grad_ref,
            grad_land.at[off - 1],
            x_send.at[off - 1],
            x_recv.at[off - 1],
            (seq, lax.rem(mp + off, heads)),
        )

    fetches[0].wait()
    for off in sorted(range(1, heads), key=lambda d: -min(d, heads - d)):
        grad_copy(off).start()
        sent.append(grad_copy(off).wait_send)
    for d in range(1, n):
        pl.semaphore_signal(
            ready, inc=1, device_id=((ys[d] * n + z) * 2 + core, mp), device_id_type=MESH
        )
    fetches[2].wait()

    def cid_copy(i, of):
        return copy_to(
            cid_ref.at[of], cid_ref.at[of], c_send.at[i], c_recv.at[i], (in_pair(*pair[i]), mp)
        )

    for i in range(3):
        cid_copy(i, mine).start()
        sent.append(cid_copy(i, mine).wait_send)

    cid_row = cid_ref[mine]
    slot_row = slots(cid_row)[0]
    target_row = cid_row * MOST + slot_row
    r_col = iota((rows, 1), 0)
    key_col = (r_col // MESSAGE) * MOST + r_col % MOST
    kind_col = r_col // MOST % KINDS
    for i in range(3, 6):
        fetches[i].wait()
    total = None
    for kind in range(3):
        chosen = as_bf16(jnp.where(kind_col == kind, key_col, -1) == target_row)
        term = dot(chosen, qkv_ref[kind])
        total = term if total is None else total + term
    packed[...] = total
    pick[...] = as_bf16(jnp.where(kind_col == 3, key_col, -1) == target_row)

    def w_part(owner):
        return w_ref[:, pl.ds(pl.multiple_of(owner * cols, cols), cols)]

    fetches[1].wait()
    head_grad = dot(grad_ref[...], w_part(mp), NT)
    for off in sorted(range(1, heads), key=lambda d: min(d, heads - d)):
        grad_copy(off).wait_recv()
        head_grad += dot(grad_land[off - 1], w_part(lax.rem(mp + heads - off, heads)), NT)
    filled = packed[...] + dot(pick[...], head_grad.astype(BF16))
    send1[...] = filled.reshape(clusters, MESSAGE, head_dim).astype(BF16)
    pl.semaphore_wait(ready, n - 1)

    def to_owner(to):
        copy_to(
            send1.at[to], land2.at[seq], s_send.at[0], s_recv.at[0], (to * 2, mp)
        ).start()

    for dy, dz in away:
        to_owner(ys[dy] * n + zs[dz])

    @pl.when(core == 0)
    def _():
        land2[seq] = send1[chip]

    @pl.when(core == 1)
    def _():
        to_owner(chip)

    def owner_sent():
        @pl.when(core == 0)
        def _():
            take(send1.at[pl.ds(0, clusters - 1)], s_send.at[0])

        @pl.when(core == 1)
        def _():
            take(send1, s_send.at[0])

    sent.append(owner_sent)

    fetches[6].wait()
    wide = 2 * FEATS * n
    half = wide // 2
    out_row = iota((wide, wide), 0)
    in_row = iota((wide, wide), 1)
    out_at = out_row % half
    wanted = (out_at // FEATS) * 2 * FEATS + (out_row // half) * FEATS + out_at % FEATS
    order = as_bf16(wanted == in_row)
    blocks = cols // wide
    for i in range(blocks):
        done = dot(order, input_ref[:, i * wide : (i + 1) * wide], NT).astype(BF16)
        piece[i] = done.reshape(2, n, FEATS, tokens)

    for i, (rows_on, cores_on) in enumerate(pair):
        cid_copy(
            i, (row + rows_on * (1 - 2 * row)) * 2 + core + cores_on * (1 - 2 * core)
        ).wait_recv()
    home_rows = clusters // 2 * 4 * MOST
    r_row = iota((1, home_rows), 1)
    key_row = r_row // (4 * MOST) * 8 * MOST + r_row % (4 * MOST)
    for of in range(4):
        _, cid_col, slot_col = slots(cid_ref[of])
        wanted = (cid_col * 4 + of) * MOST + slot_col
        for which in range(2):
            unpick[which, of * tokens : (of + 1) * tokens] = as_bf16(
                key_row + 4 * MOST * which == wanted
            )

    def input_copy(off, to, received_of=None):
        at = (
            lax.rem(mp + heads - off, heads) if received_of is not None else mp
        )
        of = mine if received_of is None else received_of
        dst = turned0.at[of, at] if to % 2 == 0 else turned1.at[of, :, at]
        return copy_to(
            piece.at[to // 2, to % 2],
            dst,
            i_send.at[4 * off + to],
            i_recv.at[4 * off + of],
            ((((y // 2) * 2 + to // 2) * n + z) * 2 + to % 2, lax.rem(mp + off, heads)),
        )

    def inputs(act):
        for off in range(heads):
            for to in range(4):
                if off == 0:

                    @pl.when(mine != to)
                    def _():
                        act(off, to)
                else:
                    act(off, to)

    inputs(lambda off, to: input_copy(off, to).start())
    sent.append(lambda: inputs(lambda off, to: input_copy(off, to).wait_send()))

    @pl.when(core == 0)
    def _():
        turned0[mine, mp] = piece[row, 0]

    @pl.when(core == 1)
    def _():
        turned1[mine, :, mp] = piece[row, 1]

    count = 2 * clusters * MOST
    lot = min(256, 2 * rows)
    part = lot // KINDS
    lots = 2 * rows // lot
    out_row = iota((lot, lot), 0)
    in_row = iota((lot, lot), 1)

    def source(p):
        first = p // (4 * MOST * n)
        second = p // (4 * MOST) % n
        return ((first * 2 + p // (2 * MOST) % 2) * n + second) * 2 * MOST + p % (2 * MOST)

    token = source(out_row % part)
    wanted = (token // MOST) * MESSAGE + (out_row // part) * MOST + token % MOST
    split_ref[...] = as_bf16(wanted == in_row)
    mask_ref[...] = jnp.where(
        source(iota((count, 1), 0)) <= source(iota((1, count), 1)), 0.0, -1e30
    )

    @pl.when(core == 0)
    def _():
        take(land2.at[pl.ds(0, 2 * clusters - 1)], s_recv.at[0])


    odd = lax.rem(chip, 2)
    even = odd == 0

    lot_home = clusters // 2
    spot = odd * lot_home + chip // 2

    def to_home(to_pair, to_y, to_z):
        copy_to(
            back1.at[to_pair * n + to_z],
            home.at[spot],
            b_send.at[0],
            b_recv.at[0],
            ((to_y * n + to_z) * 2 + odd, mp),
        ).start()

    @pl.when(core == 0)
    def _():
        got = land2[...].astype(F32).reshape(2 * rows, head_dim).astype(BF16)
        pieces = [[] for _ in range(KINDS)]
        for i in range(lots):
            parted = dot(split_ref[...], got[i * lot : (i + 1) * lot]).astype(BF16)
            for kind in range(KINDS):
                pieces[kind].append(parted[kind * part : (kind + 1) * part])
        queries, keys, values, grads = (jnp.concatenate(p, axis=0) for p in pieces)
        scores = jnp.where(mask_ref[...] < 0, -1e30, dot(keys, queries, NT) * scale)
        weights = jnp.exp(scores - jnp.max(scores, axis=0, keepdims=True))
        probs = weights / jnp.sum(weights, axis=0, keepdims=True)
        probs_low = probs.astype(BF16)
        prob_grad = dot(values, grads, NT)
        delta = jnp.sum(probs_low.astype(F32) * prob_grad, axis=0, keepdims=True)
        dscore = (probs * (prob_grad - delta)).astype(BF16)
        parts = (
            dot(dscore, keys, TN) * scale,
            dot(dscore, queries) * scale,
            dot(probs_low, grads),
        )
        for kind in range(3):
            back1[:, kind] = parts[kind].reshape(-1, 4 * MOST, head_dim).astype(BF16)

        for dy, dz in away:
            to_home(pair_rows[dy], ys[dy], zs[dz])

        @pl.when(even)
        def _():
            home[spot] = back1[y // 2 * n + z]

        @pl.when(jnp.logical_not(even))
        def _():
            to_home(y // 2, y, z)

    def back_sent():
        @pl.when((core == 0) & even)
        def _():
            take(home.at[pl.ds(0, clusters - 1)], b_send.at[0])

        @pl.when((core == 0) & jnp.logical_not(even))
        def _():
            take(home, b_send.at[0])

    sent.append(back_sent)

    @pl.when((core == 0) & even)
    def _():
        take(home.at[pl.ds(0, lot_home - 1)], b_recv.at[0])

    @pl.when((core == 1) | jnp.logical_not(even))
    def _():
        take(home.at[pl.ds(0, lot_home)], b_recv.at[0])

    own_half = pl.ds(core * lot_home, lot_home)
    other_half = pl.ds((1 - core) * lot_home, lot_home)
    swap = copy_to(home.at[own_half], home.at[own_half], h_send.at[0], h_recv.at[0], (other, mp))
    swap.start()
    sent.append(swap.wait_send)

    def order_half(which, span, kind):
        got = home[span, kind].astype(F32).reshape(home_rows, head_dim).astype(BF16)
        return dot(unpick[which], got)

    first_half = [order_half(core, own_half, kind) for kind in range(3)]
    take(home.at[pl.ds(0, lot_home)], h_recv.at[0])

    for kind in range(3):
        ordered = first_half[kind] + order_half(1 - core, other_half, kind)
        both_ref[:, kind * head_dim : (kind + 1) * head_dim] = ordered.astype(BF16)
    for which in range(2):

        @pl.when(core == which)
        def _():
            for off in range(heads):
                for of in range(4):
                    if off or of % 2 != which:
                        input_copy(off, which, of).wait_recv()
                    else:

                        @pl.when(row != of // 2)
                        def _():
                            input_copy(off, which, of).wait_recv()

    class Sums:
        def __init__(self, which):
            in_y = (n // 2, pair_rows, lambda i: ((i * 2 + row) * n + z) * 2 + which)
            in_z = (n, zs, lambda i: (y * n + i) * 2 + which)
            self.first, self.second = (in_y, in_z) if which == 0 else (in_z, in_y)
            self.turned = (turned0, turned1)[which]
            self.part_send = (part_send0, part_send1)[which]
            self.part_land = (part_land0, part_land1)[which]
            self.part_sum = (part_sum0, part_sum1)[which]
            self.last_send = (last_send0, last_send1)[which]
            self.last_land = (last_land0, last_land1)[which]

        @staticmethod
        def places(axis):
            size, near, _ = axis
            steps = [rem_at(near, size, d) for d in range(size)]
            far = sorted(range(1, size), key=lambda d: -min(d, size - d))
            return [(d, steps[d], steps[size - d]) for d in far], steps[0]

        def part_copy(self, d, to, source):
            return copy_to(
                self.part_send.at[to],
                self.part_land.at[source],
                p_send.at[d],
                p_recv.at[d],
                (self.first[2](to), mp),
            )

        def last_copy(self, d, to, source):
            return copy_to(
                self.last_send.at[to],
                self.last_land.at[source],
                l_send.at[d],
                l_recv.at[d],
                (self.second[2](to), mp),
            )

        def partial(self, to, both):
            high = self.part_send.shape[1]
            left = [self.turned[of, to].reshape(high, tokens) for of in range(4)]
            return dot(jnp.concatenate(left, axis=1), both)

        def begin(self):
            both = both_ref[...]
            others, here = self.places(self.first)
            for d, to, _ in others:
                self.part_send[to] = self.partial(to, both).astype(BF16)
                self.part_copy(d, to, here).start()
            self.part_sum[...] = self.partial(here, both).reshape(self.part_sum.shape)

        def finish(self):
            others, here = self.places(self.first)
            for d, _, source in reversed(others):
                self.part_copy(d, here, source).wait_recv()
                self.part_sum[...] += (
                    self.part_land[source].astype(F32).reshape(self.part_sum.shape)
                )
            self.last_send[...] = self.part_sum[...].astype(BF16)
            lasts, last_here = self.places(self.second)
            for d, to, _ in lasts:
                self.last_copy(d, to, last_here).start()
            wg_out[...] = self.part_sum[last_here]
            for d, to, _ in others:
                self.part_copy(d, to, here).wait_send()
            for d, _, source in reversed(lasts):
                self.last_copy(d, last_here, source).wait_recv()
                wg_out[...] += self.last_land[source].astype(F32)
            for d, to, _ in lasts:
                self.last_copy(d, to, last_here).wait_send()

    def rem_at(near, size, d):
        return near[d] if size == n else near[2 * d]

    for which in range(2):

        @pl.when(core == which)
        def _():
            Sums(which).begin()

    for kind in range(3):
        span = slice(kind * head_dim, (kind + 1) * head_dim)
        grads_out[kind] = both_ref[pl.ds(pl.multiple_of(mine * tokens, tokens), tokens), span]
    for wait_sent in sent:
        wait_sent()

    for which in range(2):

        @pl.when(core == which)
        def _():
            Sums(which).finish()


def hand_out(grads_in, wg_in, dq_out, dk_out, dv_out, wg_out, sem):
    copies = [
        pltpu.make_async_copy(grads_in.at[pl.ds(kind, 1)], out, sem.at[kind])
        for kind, out in enumerate((dq_out, dk_out, dv_out))
    ]
    copies.append(pltpu.make_async_copy(wg_in, wg_out, sem.at[3]))
    for copy in copies:
        copy.start()
    for copy in copies:
        copy.wait()


def on_device(layer_input, output_grad, w_out, query_heads, key_heads, value_heads, cluster_ids):
    devices = lax.axis_size("seq")
    heads = lax.axis_size("mp")
    n = math.isqrt(devices // 2)
    tokens, cols = layer_input.shape
    head_dim = query_heads.shape[2]
    clusters = n * n
    rows = clusters * MESSAGE
    half = FEATS * n
    lot = min(256, 2 * rows)
    width = 3 * head_dim
    vmem = pl.BlockSpec(memory_space=pltpu.VMEM)
    hbm = pl.BlockSpec(memory_space=pltpu.HBM)
    dma = pltpu.SemaphoreType.DMA
    grad_shape = jax.ShapeDtypeStruct((1, tokens, head_dim), BF16)
    wg_shape = jax.ShapeDtypeStruct((FEATS, width), F32)
    grads, weight_grad = pl.pallas_call(
        lambda *refs: kernel(n, heads, *refs),
        out_shape=(
            pltpu.VMEM((3, tokens, head_dim), BF16),
            pltpu.VMEM((FEATS, width), F32),
        ),
        in_specs=[hbm] * 7,
        out_specs=(vmem, vmem),
        scratch_shapes=[
            pltpu.VMEM((tokens, cols), BF16),
            pltpu.VMEM((tokens, cols), BF16),
            pltpu.VMEM((head_dim, heads * cols), BF16),
            pltpu.VMEM((3, tokens, head_dim), BF16),
            pltpu.VMEM((4, 1, tokens), jnp.int32),
            dma((7,)),
            pltpu.SemaphoreType.REGULAR,
            pltpu.VMEM((heads - 1, tokens, cols), BF16),
            pltpu.VMEM((rows, tokens), BF16),
            pltpu.VMEM((2, 4 * tokens, rows // 2), BF16),
            pltpu.VMEM((rows, head_dim), F32),
            pltpu.VMEM((lot, lot), BF16),
            pltpu.VMEM((2 * clusters * MOST, 2 * clusters * MOST), F32),
            pltpu.VMEM((clusters, MESSAGE, head_dim), BF16),
            pltpu.VMEM((2 * clusters, MESSAGE, head_dim), BF16),
            pltpu.VMEM((clusters // 2, 3, 4 * MOST, head_dim), BF16),
            pltpu.VMEM((clusters, 3, 4 * MOST, head_dim), BF16),
            pltpu.VMEM((2, 2, n, FEATS, tokens), BF16),
            pltpu.VMEM((4, n // 2, n, FEATS, tokens), BF16),
            pltpu.VMEM((4, n, n // 2, FEATS, tokens), BF16),
            pltpu.VMEM((4 * tokens, width), BF16),
            pltpu.VMEM((n // 2, half, width), BF16),
            pltpu.VMEM((n, half // 2, width), BF16),
            pltpu.VMEM((n // 2, half, width), BF16),
            pltpu.VMEM((n, half // 2, width), BF16),
            pltpu.VMEM((n, FEATS, width), F32),
            pltpu.VMEM((n // 2, FEATS, width), F32),
            pltpu.VMEM((n, FEATS, width), BF16),
            pltpu.VMEM((n // 2, FEATS, width), BF16),
            pltpu.VMEM((n, FEATS, width), BF16),
            pltpu.VMEM((n // 2, FEATS, width), BF16),
            dma((3,)),
            dma((3,)),
            dma((heads - 1,)),
            dma((heads - 1,)),
            dma((4 * heads,)),
            dma((4 * heads,)),
            dma((1,)),
            dma((1,)),
            dma((1,)),
            dma((1,)),
            dma((1,)),
            dma((1,)),
            dma((n,)),
            dma((n,)),
            dma((n,)),
            dma((n,)),
        ],
        compiler_params=pltpu.CompilerParams(
            collective_id=0, has_side_effects=True, vmem_limit_bytes=40 * 1024 * 1024
        ),
    )(
        *(
            pltpu.with_memory_space_constraint(x, pltpu.HBM)
            for x in (
                output_grad,
                layer_input,
                w_out,
                query_heads,
                key_heads,
                value_heads,
                cluster_ids.reshape(1, tokens),
            )
        )
    )
    return pl.pallas_call(
        hand_out,
        out_shape=(grad_shape, grad_shape, grad_shape, wg_shape),
        in_specs=[vmem] * 2,
        out_specs=(hbm,) * 4,
        scratch_shapes=[dma((4,))],
        compiler_params=pltpu.CompilerParams(vmem_limit_bytes=16 * 1024 * 1024),
    )(grads, weight_grad)


def solution(mesh):
    return jax.shard_map(
        on_device,
        mesh=mesh,
        in_specs=(
            P("seq", "mp"),
            P("seq", "mp"),
            P("mp", None),
            P("mp", "seq", None),
            P("mp", "seq", None),
            P("mp", "seq", None),
            P("mp", "seq", None),
        ),
        out_specs=(
            P("mp", "seq", None),
            P("mp", "seq", None),
            P("mp", "seq", None),
            P("seq", "mp"),
        ),
        check_vma=False,
    )
```
